512 devices in a mesh: group: 16 (over y, core), dev: 32 (over z, x).
Axes of the slice: x: 4, y: 8, z: 8, core: 2. Of those that a mesh axis runs over, the one named last changes fastest.
Arguments:
- prompt_cache: bfloat16 [16, 6144, 576], P('group', 'dev'), may hold values from -6 to 6
- prompt_of_group: int32 [16], replicated, may hold values from 0 to 15, each once
- queries: bfloat16 [16, 16, 4, 64, 576], P('group', None, None, 'dev'), may hold values from -12 to 12
- new_latents: bfloat16 [16, 16, 4, 576], P('group'), may hold values from -6 to 6
- value_up: bfloat16 [64, 512, 128], P('dev'), may hold values from -0.25 to 0.25
- out_weight: bfloat16 [8192, 7168], P('dev'), may hold values from -0.0625 to 0.0625
- norm_gain: bfloat16 [7168], replicated, may hold values from 0.099609375 to 1.8984375
- routes: int32 [1024, 8], P('group'), may hold values from 0 to 383, all different within a row; in each aligned block of 64 rows (0 to 63, 64 to 127, ...) at most 2 rows name the same one
- gates: float32 [1024, 8], P('group'), may hold values from 0.05 to 1
Outputs:
- slot_rows: float32 [16, 384, 2, 7168], P('group', 'dev')
- slot_gates: float32 [16, 384, 2], P('group', 'dev')
The draws below stay inside these ranges and needn't reach their ends.
Inputs may be any that keep to these rules, and one draw needn't show every extreme that they name: `routes`: within each aligned block of 64 rows (one decode group) every expert is named by at most 2 rows, a bound that some block reaches; a row names 8 different experts. `prompt_of_group`: each prompt is served by exactly one decode group.
All inputs are finite; a program needn't handle non-finite values.
Results may differ from the reference program's by a relative error of at most 0.015.
Values may be sent and summed in bfloat16 or wider, within the bound.
No kernel may reach another device: no remote copies, remote signals or barrier semaphores. Data moves between devices by JAX's collectives and lax.ppermute only.
A program may use at most 64 MiB of HBM per device.

```python
import math
import jax
import jax.numpy as jnp
import numpy as np
from jax import lax

D = 7168
HEADS = 64
LAT_KV = 512
HEAD_V = 128
QK_DIM = 192
EXPERTS = 384
TOP = 8
SAMPLES = 16
STEPS = 4
CAP = 2
LAT = 576
LEN = 6144
PROMPTS = 16
GROUP_ROWS = 64
ROWS = 1024


def draw_prompt_cache(key, part):
    key = jax.random.fold_in(key, 11)
    shape = (PROMPTS, LEN, LAT)
    values = jnp.clip(jax.random.normal(key, shape, jnp.float32), -6.0, 6.0)
    return values.astype(jnp.bfloat16)


def draw_queries(key, part):
    key = jax.random.fold_in(key, 13)
    shape = (PROMPTS, SAMPLES, STEPS, HEADS, LAT)
    values = jnp.clip(jax.random.normal(key, shape, jnp.float32), -6.0, 6.0)
    return values.astype(jnp.bfloat16)


def levels(own_key, dims, shards, smallest, high):
    gain, own = 1.0, jax.random.fold_in(own_key, 6)
    for dim, shards_of in shards:
        steps = jnp.exp(jax.random.uniform(jax.random.fold_in(own, dim), (shards_of,), jnp.float32, smallest / len(shards), high / len(shards)))
        gain = gain * jnp.repeat(steps, dims[dim] // shards_of).reshape([-1 if axis == dim else 1 for axis in range(len(dims))])
    return gain


def assign_block(key, own, number, rows, number_of, top, reach, slope):
    order = jax.random.permutation(key, number_of)
    crowded, common = load_shares(number_of, rows * top, reach, slope, True), load_shares(number_of, rows * top, reach, slope, False)
    places = jnp.arange(number_of)

    def named(lengths, rotation):
        used = int((lengths > 0).sum())
        fixed = max(1, used // 4)
        moved = fixed + (places - fixed + rotation * (used - fixed)) % max(1, number_of - fixed)
        return jnp.zeros((number_of,), jnp.int32).at[order[jnp.where(places < fixed, places, moved)]].set(jnp.asarray(lengths, jnp.int32))

    lengths = jnp.where(number % 4 == 0, named(crowded, number // 4), named(common, number - number // 4 - 1))
    mixed = jax.random.permutation(jax.random.fold_in(own, 3), number_of)
    donor, taker = mixed[0:number_of // 2 * 2:2], mixed[1:number_of // 2 * 2:2]
    margin = jnp.minimum(lengths[donor] - 1, reach - lengths[taker]) // 2
    margin = jnp.where((donor == order[0]) | (taker == order[0]) | (lengths[taker] == 0), 0, jnp.maximum(margin, 0))
    moved = jax.random.randint(jax.random.fold_in(own, 4), (number_of // 2,), 0, 1 << 20) % (margin + 1)
    lengths = lengths.at[donor].add(-moved).at[taker].add(moved)
    members = jnp.searchsorted(jnp.cumsum(lengths), jnp.arange(rows * top), side="right").astype(jnp.int32)
    listing = members.reshape(top, rows).T
    listing = listing[jax.random.permutation(jax.random.fold_in(own, 1), rows)]
    rotation = jax.random.randint(jax.random.fold_in(own, 2), (rows, 1), 0, top)
    return jnp.take_along_axis(listing, (jnp.arange(top)[None, :] + rotation) % top, axis=1)


def load_shares(count, total, most, slope, full):
    portions = [(1 << 20) // math.isqrt(standing ** slope) + 1 for standing in range(1, count + 1)]
    largest = most if full else min(most, max(-(-total // count), total * portions[0] // sum(portions)))
    least = 1 if total - largest >= count - 1 else 0
    counts, surplus = [largest] + [least] * (count - 1), total - largest - least * (count - 1)
    while surplus > 0:
        movable = [i for i in range(1, count) if counts[i] < largest] or [i for i in range(1, count) if counts[i] < most]
        pool, left = sum([portions[i] for i in movable]), surplus
        for i in movable:
            more = min(most - counts[i], max(1, left * portions[i] // pool), surplus)
            counts[i] = counts[i] + more
            surplus = surplus - more
    return np.array(counts)


def bell_draw(stream_key, dims, width, bound, shards=(), kind=jnp.bfloat16):
    gain = levels(stream_key, dims, shards, -0.22, 0.18) if shards else 1.0
    result = jax.random.normal(stream_key, dims, jnp.float32) * width * gain
    return jnp.minimum(jnp.maximum(result, -bound), bound).astype(kind)


def setup_inputs(seed: int = 0) -> dict:
    seeds = jax.random.split(jax.random.key(seed), 10)
    prompt_cache = draw_prompt_cache(jax.random.fold_in(seeds[9], 71), 0)
    prompt_of_group = jax.random.permutation(seeds[1], PROMPTS).astype(jnp.int32)
    queries = draw_queries(jax.random.fold_in(seeds[9], 71), 0)
    new_latents = bell_draw(seeds[3], (PROMPTS, SAMPLES, STEPS, LAT), 1.0, 6.0, ((0, 16),))
    value_up = bell_draw(seeds[4], (HEADS, LAT_KV, HEAD_V), LAT_KV ** -0.5, 0.25, ((0, 32),))
    out_weight = bell_draw(seeds[5], (HEADS * HEAD_V, D), (HEADS * HEAD_V) ** -0.5, 0.0625, ((0, 32),))
    norm_gain = jnp.clip(1.0 + 0.18 * jax.random.normal(seeds[6], (D,), jnp.float32), 0.099609375, 1.8984375).astype(jnp.bfloat16)
    routes_keys = jax.random.split(jax.random.fold_in(seeds[7], 1), ROWS // GROUP_ROWS)
    routes_turns = jax.random.permutation(jax.random.fold_in(seeds[7], 3), ROWS // GROUP_ROWS)
    routes = jax.vmap(lambda own, number: assign_block(jax.random.fold_in(seeds[7], 2), own, number, GROUP_ROWS, EXPERTS, TOP, CAP, 2))(routes_keys, routes_turns).reshape((ROWS, TOP))
    gates = jnp.clip(jnp.exp(math.log(1.0) - 2.9957323 * jax.random.uniform(seeds[8], (ROWS, TOP), jnp.float32) ** levels(seeds[8], (ROWS, TOP), ((0, 16),), -0.2, 0.2)), 0.05, 1.0)
    return {"prompt_cache": prompt_cache, "prompt_of_group": prompt_of_group, "queries": queries, "new_latents": new_latents, "value_up": value_up, "out_weight": out_weight, "norm_gain": norm_gain, "routes": routes, "gates": gates}


EPSILON = 1e-06

def one_group(group_id, prompt_cache, prompt_of_group, queries, new_latents, value_up, out_weight, norm_gain, routes, gates):
    scale = QK_DIM ** (-0.5)
    cache = prompt_cache[prompt_of_group[group_id]].astype(jnp.float32)
    query_rows = queries[group_id].astype(jnp.float32)
    own_rows = new_latents[group_id].astype(jnp.float32)
    prompt_scores = jnp.einsum('sthc,nc->sthn', query_rows, cache) * scale
    own_scores = jnp.einsum('sthc,suc->sthu', query_rows, own_rows) * scale
    steps_index = jnp.arange(STEPS, dtype=jnp.int32)
    visible = steps_index[None, :] <= steps_index[:, None]
    own_scores = jnp.where(visible[None, :, None, :], own_scores, -1e+30)
    top_score = jnp.maximum(lax.optimization_barrier(jnp.max(prompt_scores, axis=-1)), lax.optimization_barrier(jnp.max(own_scores, axis=-1)))
    prompt_weights = jnp.exp(prompt_scores - top_score[..., None])
    own_weights = jnp.exp(own_scores - top_score[..., None])
    total = lax.optimization_barrier(jnp.sum(prompt_weights, axis=-1)) + lax.optimization_barrier(jnp.sum(own_weights, axis=-1))
    numer = jnp.einsum('sthn,nc->sthc', prompt_weights.astype(jnp.bfloat16).astype(jnp.float32), cache[:, :LAT_KV])
    numer = numer + jnp.einsum('sthu,suc->sthc', own_weights.astype(jnp.bfloat16).astype(jnp.float32), own_rows[..., :LAT_KV])
    latent_out = (numer / total[..., None]).astype(jnp.bfloat16)
    head_values = jnp.einsum('sthc,hcv->sthv', latent_out.astype(jnp.float32), value_up.astype(jnp.float32)).astype(jnp.bfloat16)
    attention = jnp.dot(head_values.reshape(GROUP_ROWS, HEADS * HEAD_V), out_weight, preferred_element_type=jnp.float32)
    mean_square = lax.optimization_barrier(jnp.mean(attention * attention, axis=-1, keepdims=True))
    normed = attention * lax.rsqrt(mean_square + EPSILON) * norm_gain.astype(jnp.float32)
    first_row = (group_id * GROUP_ROWS).astype(jnp.int32)
    group_routes = lax.dynamic_slice_in_dim(routes, first_row, GROUP_ROWS, 0)
    group_gates = lax.dynamic_slice_in_dim(gates, first_row, GROUP_ROWS, 0)
    matches = (group_routes[:, :, None] == jnp.arange(EXPERTS, dtype=jnp.int32)[None, None, :]).astype(jnp.float32)
    chosen = lax.optimization_barrier(jnp.sum(matches, axis=1))
    gating = lax.optimization_barrier(jnp.sum(matches * group_gates[:, :, None], axis=1))
    position = jnp.cumsum(chosen, axis=0) - chosen
    slot_index = jnp.arange(CAP, dtype=jnp.float32)
    selected = chosen[:, :, None] * (position[:, :, None] == slot_index[None, None, :]).astype(jnp.float32)
    slot_rows = jnp.einsum('rec,rd->ecd', selected, normed, precision=lax.Precision.HIGHEST)
    slot_gates = jnp.einsum('rec,re->ec', selected, gating, precision=lax.Precision.HIGHEST)
    return (slot_rows, slot_gates)

def reference(prompt_cache, prompt_of_group, queries, new_latents, value_up, out_weight, norm_gain, routes, gates):

    def apply(group_id):
        return one_group(group_id, prompt_cache, prompt_of_group, queries, new_latents, value_up, out_weight, norm_gain, routes, gates)
    slot_rows, slot_gates = lax.map(apply, jnp.arange(PROMPTS, dtype=jnp.int32))
    return (slot_rows, slot_gates)
```

```python
import jax
import jax.numpy as jnp
from jax import lax
from jax.experimental import pallas as pl
from jax.experimental.pallas import tpu as pltpu
from jax.sharding import Mesh
from jax.sharding import PartitionSpec as P

D = 7168
LAT = 576
LAT_KV = 512
HEAD_V = 128
QK_DIM = 192
EXPERTS = 384
CAP = 2
ROWS = 64
EPSILON = 1e-06
SCALE = QK_DIM ** (-0.5)

NY, NZ, NX = 8, 8, 4
DEVS = NZ * NX
PIECE = 192 // NY
KEYS = 192 * NX
MINE = 2 * ROWS
SENT = MINE + 16
SLOTS = EXPERTS * CAP
OWN_SLOTS = SLOTS // DEVS
QUARTER = D // NX
BLOCK = 256
BLOCKS = QUARTER // BLOCK

bf16 = jnp.bfloat16
f32 = jnp.float32
VMEM = pl.BlockSpec(memory_space=pltpu.VMEM)
SMEM = pl.BlockSpec(memory_space=pltpu.SMEM)


def params():
    return pltpu.CompilerParams(vmem_limit_bytes=48 * 1024 * 1024)


def dot(a, b, dims=((1,), (0,))):
    return lax.dot_general(a, b, (dims, ((), ())), preferred_element_type=f32)


def columns_to_lanes(column):
    return jnp.transpose(jnp.broadcast_to(column, (MINE, 128)))[:1]


def pick_kernel(wanted, mine, other, out):
    core = wanted[8]
    for y in range(NY):
        prompt = wanted[y]
        row = lax.shift_right_logical(prompt, 1)

        @pl.when((prompt & 1) == core)
        def _():
            out[y] = mine[row]

        @pl.when((prompt & 1) != core)
        def _():
            out[y] = other[row]


def pick(wanted, mine, other):
    return pl.pallas_call(
        pick_kernel,
        out_shape=jax.ShapeDtypeStruct(mine.shape, mine.dtype),
        in_specs=[SMEM, VMEM, VMEM],
        out_specs=VMEM,
        compiler_params=params(),
        name="pick",
    )(wanted, mine, other)


def attend(query, keys, visible=None):
    scores = dot(query, keys, ((1,), (1,))) * SCALE
    if visible is not None:
        scores = jnp.where(visible, scores, -1e30)
    best = jnp.max(scores, axis=1, keepdims=True)
    weights = jnp.exp(scores - best)
    total = jnp.sum(weights, axis=1, keepdims=True)
    latent = dot(weights.astype(bf16), keys[:, :LAT_KV]) / total
    return best, total, latent.astype(bf16)


def three(value):
    high = value.astype(bf16).astype(f32)
    rest = value - high
    mid = rest.astype(bf16).astype(f32)
    return high, mid, rest - mid


def attention_kernel(query, keys, value_up, out):
    best, total, latent = attend(query[0], keys[...])
    for head in range(2):
        values = dot(latent[head * ROWS : (head + 1) * ROWS], value_up[0, head])
        out[0, head * ROWS : (head + 1) * ROWS, :] = values.astype(bf16)
    parts = three(columns_to_lanes(best)) + three(columns_to_lanes(total))
    index = lax.broadcasted_iota(jnp.int32, (16, 128), 0)
    stats = jnp.zeros((16, 128), f32)
    for i, part in enumerate(parts):
        stats = jnp.where(index == i, jnp.broadcast_to(part, (16, 128)), stats)
    out[0, MINE:, :] = stats.astype(bf16)


def prompt_attention(queries, keys, value_up):
    return pl.pallas_call(
        attention_kernel,
        grid=(NZ,),
        out_shape=jax.ShapeDtypeStruct((NZ, SENT, 128), bf16),
        in_specs=[
            pl.BlockSpec((1, MINE, LAT), lambda z: (z, 0, 0)),
            pl.BlockSpec((KEYS, LAT), lambda z: (0, 0)),
            pl.BlockSpec((1, 2, LAT_KV, HEAD_V), lambda z: (z, 0, 0, 0)),
        ],
        out_specs=pl.BlockSpec((1, SENT, 128), lambda z: (z, 0, 0)),
        compiler_params=params(),
        name="prompt_attention",
    )(queries, keys, value_up)


def own_kernel(query, keys, value_up, values, stats):
    row = lax.broadcasted_iota(jnp.int32, (MINE, ROWS), 0) & (ROWS - 1)
    key = lax.broadcasted_iota(jnp.int32, (MINE, ROWS), 1)
    same = lax.shift_right_logical(row, 2) == lax.shift_right_logical(key, 2)
    best, total, latent = attend(query[...], keys[...], same & (key <= row))
    for head in range(2):
        part = slice(head * ROWS, (head + 1) * ROWS)
        values[part, :] = dot(latent[part], value_up[head])
    index = lax.broadcasted_iota(jnp.int32, (8, 128), 0)
    stats[...] = jnp.where(
        index == 0,
        jnp.broadcast_to(columns_to_lanes(best), (8, 128)),
        jnp.broadcast_to(columns_to_lanes(total), (8, 128)),
    )


def own_attention(query, keys, value_up):
    return pl.pallas_call(
        own_kernel,
        out_shape=(
            jax.ShapeDtypeStruct((MINE, HEAD_V), f32),
            jax.ShapeDtypeStruct((8, 128), f32),
        ),
        in_specs=[VMEM] * 3,
        out_specs=(VMEM, VMEM),
        compiler_params=params(),
        name="own_attention",
    )(query, keys, value_up)


def combine_kernel(arrived, own_values, own_stats, out):
    bests, totals = [own_stats[0:1, :]], [own_stats[1:2, :]]
    for z in range(NZ):
        stats = arrived[z, MINE:, :].astype(f32)
        bests.append(stats[0:1] + stats[1:2] + stats[2:3])
        totals.append(stats[3:4] + stats[4:5] + stats[5:6])
    top = bests[0]
    for best in bests[1:]:
        top = jnp.maximum(top, best)
    shares = [total * jnp.exp(best - top) for best, total in zip(bests, totals)]
    whole = shares[0]
    for share in shares[1:]:
        whole = whole + share
    index = lax.broadcasted_iota(jnp.int32, (128, 128), 0)
    table = jnp.zeros((128, 128), f32)
    for i, share in enumerate(shares):
        table = jnp.where(index == i, jnp.broadcast_to(share / whole, (128, 128)), table)
    table = jnp.transpose(table)
    values = table[:, 0:1] * own_values[...]
    for z in range(NZ):
        values = values + table[:, z + 1 : z + 2] * arrived[z, :MINE, :].astype(f32)
    values = values.astype(bf16)
    for x in range(NX):
        out[x, :, :HEAD_V] = values[:ROWS]
        out[x, :, HEAD_V:] = values[ROWS:]


def combine(arrived, own_values, own_stats):
    return pl.pallas_call(
        combine_kernel,
        out_shape=jax.ShapeDtypeStruct((NX, ROWS, 2 * HEAD_V), bf16),
        in_specs=[VMEM] * 3,
        out_specs=VMEM,
        compiler_params=params(),
        name="combine",
    )(arrived, own_values, own_stats)


def project_kernel(head_values, weight, out):
    @pl.when(pl.program_id(0) < BLOCKS)
    def _():
        total = dot(head_values[0], weight[0])
        for x in range(1, NX):
            total = total + dot(head_values[x], weight[x])
        out[0] = total.astype(bf16)

    @pl.when(pl.program_id(0) >= BLOCKS)
    def _():
        out[0] = jnp.zeros((ROWS, BLOCK), bf16)


def project(head_values, weight):
    return pl.pallas_call(
        project_kernel,
        grid=(NZ,),
        out_shape=jax.ShapeDtypeStruct((NZ, ROWS, BLOCK), bf16),
        in_specs=[
            pl.BlockSpec((NX, ROWS, 2 * HEAD_V), lambda z: (0, 0, 0)),
            pl.BlockSpec((NX, 2 * HEAD_V, BLOCK), lambda z: (0, 0, jnp.minimum(z, BLOCKS - 1))),
        ],
        out_specs=pl.BlockSpec((1, ROWS, BLOCK), lambda z: (z, 0, 0)),
        compiler_params=params(),
        name="project",
    )(head_values, weight)


def slots_kernel(routes, gates, picks, slot_gates):
    slot = lax.broadcasted_iota(jnp.int32, (SLOTS, ROWS), 0)
    expert = lax.shift_right_logical(slot, 1)
    chosen = jnp.zeros((SLOTS, ROWS), f32)
    gating = jnp.zeros((SLOTS, ROWS), f32)
    for k in range(8):
        match = expert == routes[k : k + 1, :]
        chosen = jnp.where(match, 1.0, chosen)
        gating = jnp.where(match, gates[k : k + 1, :], gating)
    earlier = lax.broadcasted_iota(jnp.int32, (ROWS, ROWS), 0) < lax.broadcasted_iota(
        jnp.int32, (ROWS, ROWS), 1
    )
    position = dot(chosen.astype(bf16), jnp.where(earlier, 1.0, 0.0).astype(bf16))
    place = (slot & 1).astype(f32)
    selected = jnp.where(position == place, chosen, 0.0)
    picks[...] = selected.astype(bf16)
    slot_gates[...] = jnp.sum(selected * gating, axis=1, keepdims=True)


def slots(routes, gates):
    return pl.pallas_call(
        slots_kernel,
        out_shape=(
            jax.ShapeDtypeStruct((SLOTS, ROWS), bf16),
            jax.ShapeDtypeStruct((SLOTS, 1), f32),
        ),
        in_specs=[VMEM] * 2,
        out_specs=(VMEM, VMEM),
        compiler_params=params(),
        name="slots",
    )(routes, gates)


def dispatch_kernel(arrived, picks, out):
    total = arrived[0].astype(f32)
    for z in range(1, NZ):
        total = total + arrived[z].astype(f32)
    out[...] = dot(picks[...], total.astype(bf16)).astype(bf16)


def dispatch(arrived, picks):
    return pl.pallas_call(
        dispatch_kernel,
        out_shape=jax.ShapeDtypeStruct((SLOTS, BLOCK), bf16),
        in_specs=[VMEM] * 2,
        out_specs=VMEM,
        compiler_params=params(),
        name="dispatch",
    )(arrived, picks)


def norm_kernel(arrived, gain, out):
    blocks = []
    for x in range(NX):
        for z in range(BLOCKS):
            blocks.append(arrived[z * NX + x].astype(f32))
    square = blocks[0] * blocks[0]
    for block in blocks[1:]:
        square = square + block * block
    scale = lax.rsqrt(jnp.sum(square, axis=1, keepdims=True) * (1.0 / D) + EPSILON)
    for i, block in enumerate(blocks):
        part = slice(i * BLOCK, (i + 1) * BLOCK)
        normed = block * scale * gain[:, part].astype(f32)
        for expert in range(OWN_SLOTS // CAP):
            out[expert, :, part] = normed[expert * CAP : (expert + 1) * CAP]


def norm(arrived, gain):
    return pl.pallas_call(
        norm_kernel,
        out_shape=jax.ShapeDtypeStruct((OWN_SLOTS // CAP, CAP, D), f32),
        in_specs=[VMEM] * 2,
        out_specs=VMEM,
        compiler_params=params(),
        name="norm",
    )(arrived, gain)


def exchange(value, axes):
    return lax.all_to_all(value, axes, split_axis=0, concat_axis=0, tiled=True)


def local(
    prompt_cache,
    prompt_of_group,
    queries,
    new_latents,
    value_up,
    out_weight,
    norm_gain,
    routes,
    gates,
):
    core = lax.axis_index("core")
    dev = lax.axis_index("z") * NX + lax.axis_index("x")

    pieces = exchange(prompt_cache.reshape(NY, PIECE, LAT), "y")
    other = lax.ppermute(pieces, "core", [(0, 1), (1, 0)])
    own_prompts = jnp.where(core == 0, prompt_of_group[0::2], prompt_of_group[1::2])
    wanted = jnp.concatenate([own_prompts, core[None].astype(jnp.int32)])
    served = exchange(pick(wanted, pieces, other), "y").reshape(NY * PIECE, LAT)
    keys = lax.all_gather(served, "x", axis=0, tiled=True)

    query = queries.reshape(ROWS, 2, LAT).transpose(1, 0, 2).reshape(MINE, LAT)
    all_queries = exchange(jnp.broadcast_to(query, (NZ, MINE, LAT)), "z")
    all_value_up = lax.all_gather(
        value_up.reshape(2 * LAT_KV, HEAD_V), "z", axis=0, tiled=True
    ).reshape(NZ, 2, LAT_KV, HEAD_V)
    weight = exchange(out_weight.reshape(2 * HEAD_V, NX, QUARTER).transpose(1, 0, 2), "x")
    own_values, own_stats = own_attention(query, new_latents.reshape(ROWS, LAT), value_up)
    picks, all_gates = slots(routes.T, gates.T)
    slot_gates = lax.dynamic_slice_in_dim(all_gates, dev * OWN_SLOTS, OWN_SLOTS, 0)

    partial = exchange(prompt_attention(all_queries, keys, all_value_up), "z")
    head_values = exchange(combine(partial, own_values, own_stats), "x")
    sums = exchange(project(head_values, weight), "z")
    rows = dispatch(sums, picks).reshape(DEVS, OWN_SLOTS, BLOCK)
    slot_rows = norm(exchange(rows, ("z", "x")), norm_gain.reshape(1, D))
    return (slot_rows[None], slot_gates.reshape(1, OWN_SLOTS // CAP, CAP))


def solution(mesh):
    fine = Mesh(mesh.devices.reshape(NY, 2, NZ, NX), ("y", "core", "z", "x"))
    group, dev = ("y", "core"), ("z", "x")
    return jax.shard_map(
        local,
        mesh=fine,
        in_specs=(
            P(group, dev, None),
            P(),
            P(group, None, None, dev, None),
            P(group, None, None, None),
            P(dev, None, None),
            P(dev, None),
            P(),
            P(group, None),
            P(group, None),
        ),
        out_specs=(P(group, dev, None, None), P(group, dev, None)),
        check_vma=False,
    )
```

```python
import jax
import jax.numpy as jnp
from jax import lax
from jax.experimental import pallas as pl
from jax.experimental.pallas import tpu as pltpu
from jax.sharding import Mesh
from jax.sharding import PartitionSpec as P

D = 7168
LAT = 576
LAT_KV = 512
HEAD_V = 128
QK_DIM = 192
EXPERTS = 384
CAP = 2
ROWS = 64
EPSILON = 1e-06
SCALE = QK_DIM ** (-0.5)

NY, NZ, NX = 8, 8, 4
DEVS = NZ * NX
PIECE = 192 // NY
KEYS = 192 * NX
MINE = 2 * ROWS
SENT = MINE + 16
SLOTS = EXPERTS * CAP
OWN_SLOTS = SLOTS // DEVS
QUARTER = D // NX
BLOCK = 256
BLOCKS = QUARTER // BLOCK
TILES = -(-LAT // 128)
PACKED = TILES * MINE + LAT_KV
STEP = 4

bf16 = jnp.bfloat16
f32 = jnp.float32
VMEM = pl.BlockSpec(memory_space=pltpu.VMEM)
SMEM = pl.BlockSpec(memory_space=pltpu.SMEM)


def params():
    return pltpu.CompilerParams(vmem_limit_bytes=24 * 1024 * 1024)


def dot(a, b, dims=((1,), (0,))):
    return lax.dot_general(a, b, (dims, ((), ())), preferred_element_type=f32)


def columns_to_lanes(column):
    return jnp.transpose(jnp.broadcast_to(column, (MINE, 128)))[:1]


def pick_kernel(wanted, mine, other, out):
    core = wanted[8]
    for y in range(NY):
        prompt = wanted[y]
        row = lax.shift_right_logical(prompt, 1)

        @pl.when((prompt & 1) == core)
        def _():
            out[y] = mine[row]

        @pl.when((prompt & 1) != core)
        def _():
            out[y] = other[row]


def pick(wanted, mine, other):
    return pl.pallas_call(
        pick_kernel,
        out_shape=jax.ShapeDtypeStruct(mine.shape, mine.dtype),
        in_specs=[SMEM, VMEM, VMEM],
        out_specs=VMEM,
        compiler_params=params(),
        name="pick",
    )(wanted, mine, other)


def attend(query, keys, visible=None):
    scores = dot(query, keys, ((1,), (1,))) * SCALE
    if visible is not None:
        scores = jnp.where(visible, scores, -1e30)
    best = jnp.max(scores, axis=1, keepdims=True)
    weights = jnp.exp(scores - best)
    total = jnp.sum(weights, axis=1, keepdims=True)
    latent = dot(weights.astype(bf16), keys[:, :LAT_KV]) / total
    return best, total, latent.astype(bf16)


def three(value):
    high = value.astype(bf16).astype(f32)
    rest = value - high
    mid = rest.astype(bf16).astype(f32)
    return high, mid, rest - mid


def pack_kernel(core, query, value_up, out):
    for tile in range(TILES):
        width = min(128, LAT - tile * 128)
        part = query[:, tile * 128 : tile * 128 + width]
        if width < 128:
            part = jnp.concatenate([part, jnp.zeros((MINE, 128 - width), bf16)], axis=1)
        out[tile * MINE : (tile + 1) * MINE, :] = part
    out[TILES * MINE :, :] = value_up[core[0]]


def pack(core, query, value_up):
    return pl.pallas_call(
        pack_kernel,
        out_shape=jax.ShapeDtypeStruct((PACKED, 128), bf16),
        in_specs=[SMEM, VMEM, VMEM],
        out_specs=VMEM,
        compiler_params=params(),
        name="pack",
    )(core, query, value_up)


def attention_kernel(packed, keys, latents, stats):
    index = lax.broadcasted_iota(jnp.int32, (16, 128), 0)
    for step in range(NZ // STEP):
        zs = range(step * STEP, (step + 1) * STEP)
        query = jnp.concatenate(
            [
                jnp.concatenate(
                    [packed[z, tile * MINE : (tile + 1) * MINE, :] for tile in range(TILES)], axis=1
                )
                for z in zs
            ],
            axis=0,
        )[:, :LAT]
        best, total, latent = attend(query, keys[...])
        for i, z in enumerate(zs):
            part = slice(i * MINE, (i + 1) * MINE)
            latents[z] = latent[part]
            rows = three(columns_to_lanes(best[part])) + three(columns_to_lanes(total[part]))
            table = jnp.zeros((16, 128), f32)
            for j, row in enumerate(rows):
                table = jnp.where(index == j, jnp.broadcast_to(row, (16, 128)), table)
            stats[z] = table.astype(bf16)


def prompt_attention(packed, keys):
    return pl.pallas_call(
        attention_kernel,
        out_shape=(
            jax.ShapeDtypeStruct((NZ, MINE, LAT_KV), bf16),
            jax.ShapeDtypeStruct((NZ, 16, 128), bf16),
        ),
        in_specs=[VMEM] * 2,
        out_specs=(VMEM, VMEM),
        compiler_params=params(),
        name="prompt_attention",
    )(packed, keys)


def up_kernel(core, latents, stats, mine, other, out):
    for z in range(NZ):
        out[z, MINE:, :] = stats[z]

    def apply(first, second):
        for z in range(NZ):
            out[z, :ROWS, :] = dot(latents[z, :ROWS], first(z)).astype(bf16)
            out[z, ROWS:MINE, :] = dot(latents[z, ROWS:], second(z)).astype(bf16)

    @pl.when(core[0] == 0)
    def _():
        apply(lambda z: mine[z, TILES * MINE :, :], lambda z: other[z])

    @pl.when(core[0] != 0)
    def _():
        apply(lambda z: other[z], lambda z: mine[z, TILES * MINE :, :])


def up_project(core, latents, stats, mine, other):
    return pl.pallas_call(
        up_kernel,
        out_shape=jax.ShapeDtypeStruct((NZ, SENT, 128), bf16),
        in_specs=[SMEM] + [VMEM] * 4,
        out_specs=VMEM,
        compiler_params=params(),
        name="up_project",
    )(core, latents, stats, mine, other)


def turn_kernel(x, weight, *refs):
    outs, sems = refs[:NX], refs[NX]
    copies = []
    for k in range(NX):
        start = pl.multiple_of(((x[0] + k) & (NX - 1)) * QUARTER, 128)
        copies.append(
            pltpu.make_async_copy(weight.at[:, pl.ds(start, QUARTER)], outs[k], sems.at[k])
        )
    for copy in copies:
        copy.start()
    for copy in copies:
        copy.wait()


def turn(x, weight):
    return pl.pallas_call(
        turn_kernel,
        out_shape=[jax.ShapeDtypeStruct((2 * HEAD_V, QUARTER), bf16)] * NX,
        in_specs=[SMEM, pl.BlockSpec(memory_space=pl.ANY)],
        out_specs=[pl.BlockSpec(memory_space=pl.ANY)] * NX,
        scratch_shapes=[pltpu.SemaphoreType.DMA((NX,))],
        compiler_params=params(),
        name="turn",
    )(x, weight)


def own_kernel(query, keys, value_up, values, stats):
    row = lax.broadcasted_iota(jnp.int32, (MINE, ROWS), 0) & (ROWS - 1)
    key = lax.broadcasted_iota(jnp.int32, (MINE, ROWS), 1)
    same = lax.shift_right_logical(row, 2) == lax.shift_right_logical(key, 2)
    best, total, latent = attend(query[...], keys[...], same & (key <= row))
    for head in range(2):
        part = slice(head * ROWS, (head + 1) * ROWS)
        values[part, :] = dot(latent[part], value_up[head])
    index = lax.broadcasted_iota(jnp.int32, (8, 128), 0)
    stats[...] = jnp.where(
        index == 0,
        jnp.broadcast_to(columns_to_lanes(best), (8, 128)),
        jnp.broadcast_to(columns_to_lanes(total), (8, 128)),
    )


def own_attention(query, keys, value_up):
    return pl.pallas_call(
        own_kernel,
        out_shape=(
            jax.ShapeDtypeStruct((MINE, HEAD_V), f32),
            jax.ShapeDtypeStruct((8, 128), f32),
        ),
        in_specs=[VMEM] * 3,
        out_specs=(VMEM, VMEM),
        compiler_params=params(),
        name="own_attention",
    )(query, keys, value_up)


def combine_kernel(arrived, own_values, own_stats, out):
    bests, totals = [own_stats[0:1, :]], [own_stats[1:2, :]]
    for z in range(NZ):
        stats = arrived[z, MINE:, :].astype(f32)
        bests.append(stats[0:1] + stats[1:2] + stats[2:3])
        totals.append(stats[3:4] + stats[4:5] + stats[5:6])
    top = bests[0]
    for best in bests[1:]:
        top = jnp.maximum(top, best)
    shares = [total * jnp.exp(best - top) for best, total in zip(bests, totals)]
    whole = shares[0]
    for share in shares[1:]:
        whole = whole + share
    index = lax.broadcasted_iota(jnp.int32, (128, 128), 0)
    table = jnp.zeros((128, 128), f32)
    for i, share in enumerate(shares):
        table = jnp.where(index == i, jnp.broadcast_to(share / whole, (128, 128)), table)
    table = jnp.transpose(table)
    values = table[:, 0:1] * own_values[...]
    for z in range(NZ):
        values = values + table[:, z + 1 : z + 2] * arrived[z, :MINE, :].astype(f32)
    values = values.astype(bf16)
    for x in range(NX):
        out[x, :, :HEAD_V] = values[:ROWS]
        out[x, :, HEAD_V:] = values[ROWS:]


def combine(arrived, own_values, own_stats):
    return pl.pallas_call(
        combine_kernel,
        out_shape=jax.ShapeDtypeStruct((NX, ROWS, 2 * HEAD_V), bf16),
        in_specs=[VMEM] * 3,
        out_specs=VMEM,
        compiler_params=params(),
        name="combine",
    )(arrived, own_values, own_stats)


def project_kernel(x, head_values, *refs):
    weights, out = refs[:NX], refs[NX]
    rows = [head_values[(x[0] + NX - k) & (NX - 1)] for k in range(NX)]
    for block in range(BLOCKS):
        part = slice(block * BLOCK, (block + 1) * BLOCK)
        total = dot(rows[0], weights[0][:, part])
        for k in range(1, NX):
            total = total + dot(rows[k], weights[k][:, part])
        out[block] = total.astype(bf16)
    for block in range(BLOCKS, NZ):
        out[block] = jnp.zeros((ROWS, BLOCK), bf16)


def project(x, head_values, weights):
    return pl.pallas_call(
        project_kernel,
        out_shape=jax.ShapeDtypeStruct((NZ, ROWS, BLOCK), bf16),
        in_specs=[SMEM] + [VMEM] * (1 + NX),
        out_specs=VMEM,
        compiler_params=params(),
        name="project",
    )(x, head_values, *weights)


def slots_kernel(routes, gates, picks, slot_gates):
    slot = lax.broadcasted_iota(jnp.int32, (SLOTS, ROWS), 0)
    expert = lax.shift_right_logical(slot, 1)
    chosen = jnp.zeros((SLOTS, ROWS), f32)
    gating = jnp.zeros((SLOTS, ROWS), f32)
    for k in range(8):
        match = expert == routes[k : k + 1, :]
        chosen = jnp.where(match, 1.0, chosen)
        gating = jnp.where(match, gates[k : k + 1, :], gating)
    earlier = lax.broadcasted_iota(jnp.int32, (ROWS, ROWS), 0) < lax.broadcasted_iota(
        jnp.int32, (ROWS, ROWS), 1
    )
    position = dot(chosen.astype(bf16), jnp.where(earlier, 1.0, 0.0).astype(bf16))
    place = (slot & 1).astype(f32)
    selected = jnp.where(position == place, chosen, 0.0)
    picks[...] = selected.astype(bf16)
    slot_gates[...] = jnp.sum(selected * gating, axis=1, keepdims=True)


def slots(routes, gates):
    return pl.pallas_call(
        slots_kernel,
        out_shape=(
            jax.ShapeDtypeStruct((SLOTS, ROWS), bf16),
            jax.ShapeDtypeStruct((SLOTS, 1), f32),
        ),
        in_specs=[VMEM] * 2,
        out_specs=(VMEM, VMEM),
        compiler_params=params(),
        name="slots",
    )(routes, gates)


def dispatch_kernel(arrived, picks, out):
    total = arrived[0].astype(f32)
    for z in range(1, NZ):
        total = total + arrived[z].astype(f32)
    out[...] = dot(picks[...], total.astype(bf16)).astype(bf16)


def dispatch(arrived, picks):
    return pl.pallas_call(
        dispatch_kernel,
        out_shape=jax.ShapeDtypeStruct((SLOTS, BLOCK), bf16),
        in_specs=[VMEM] * 2,
        out_specs=VMEM,
        compiler_params=params(),
        name="dispatch",
    )(arrived, picks)


def norm_kernel(arrived, gain, out):
    blocks = []
    for x in range(NX):
        for z in range(BLOCKS):
            blocks.append(arrived[z * NX + x].astype(f32))
    square = blocks[0] * blocks[0]
    for block in blocks[1:]:
        square = square + block * block
    scale = lax.rsqrt(jnp.sum(square, axis=1, keepdims=True) * (1.0 / D) + EPSILON)
    for i, block in enumerate(blocks):
        part = slice(i * BLOCK, (i + 1) * BLOCK)
        normed = block * scale * gain[:, part].astype(f32)
        for expert in range(OWN_SLOTS // CAP):
            out[expert, :, part] = normed[expert * CAP : (expert + 1) * CAP]


def norm(arrived, gain):
    return pl.pallas_call(
        norm_kernel,
        out_shape=jax.ShapeDtypeStruct((OWN_SLOTS // CAP, CAP, D), f32),
        in_specs=[VMEM] * 2,
        out_specs=VMEM,
        compiler_params=params(),
        name="norm",
    )(arrived, gain)


def exchange(value, axes):
    return lax.all_to_all(value, axes, split_axis=0, concat_axis=0, tiled=True)


def local(
    prompt_cache,
    prompt_of_group,
    queries,
    new_latents,
    value_up,
    out_weight,
    norm_gain,
    routes,
    gates,
):
    core = lax.axis_index("core")
    dev = lax.axis_index("z") * NX + lax.axis_index("x")

    pieces = exchange(prompt_cache.reshape(NY, PIECE, LAT), "y")
    other = lax.ppermute(pieces, "core", [(0, 1), (1, 0)])
    own_prompts = jnp.where(core == 0, prompt_of_group[0::2], prompt_of_group[1::2])
    wanted = jnp.concatenate([own_prompts, core[None].astype(jnp.int32)])
    served = exchange(pick(wanted, pieces, other), "y").reshape(NY * PIECE, LAT)
    keys = lax.all_gather(served, "x", axis=0, tiled=True)

    query = queries.reshape(ROWS, 2, LAT).transpose(1, 0, 2).reshape(MINE, LAT)
    core = core[None].astype(jnp.int32)
    x = lax.axis_index("x")[None].astype(jnp.int32)
    packed = lax.all_gather(pack(core, query, value_up), "z", axis=0, tiled=True)
    packed = packed.reshape(NZ, PACKED, 128)
    other_up = lax.ppermute(packed[:, TILES * MINE :, :], "core", [(0, 1), (1, 0)])
    weights = turn(x, out_weight)
    weights = [weights[0]] + [
        lax.ppermute(weights[k], "x", [(i, (i + k) % NX) for i in range(NX)]) for k in range(1, NX)
    ]
    own_values, own_stats = own_attention(query, new_latents.reshape(ROWS, LAT), value_up)
    picks, all_gates = slots(routes.T, gates.T)
    slot_gates = lax.dynamic_slice_in_dim(all_gates, dev * OWN_SLOTS, OWN_SLOTS, 0)

    latents, stats = prompt_attention(packed, keys)
    partial = exchange(up_project(core, latents, stats, packed, other_up), "z")
    head_values = exchange(combine(partial, own_values, own_stats), "x")
    sums = exchange(project(x, head_values, weights), "z")
    rows = dispatch(sums, picks).reshape(DEVS, OWN_SLOTS, BLOCK)
    slot_rows = norm(exchange(rows, ("z", "x")), norm_gain.reshape(1, D))
    return (slot_rows[None], slot_gates.reshape(1, OWN_SLOTS // CAP, CAP))


def solution(mesh):
    fine = Mesh(mesh.devices.reshape(NY, 2, NZ, NX), ("y", "core", "z", "x"))
    group, dev = ("y", "core"), ("z", "x")
    return jax.shard_map(
        local,
        mesh=fine,
        in_specs=(
            P(group, dev, None),
            P(),
            P(group, None, None, dev, None),
            P(group, None, None, None),
            P(dev, None, None),
            P(dev, None),
            P(),
            P(group, None),
            P(group, None),
        ),
        out_specs=(P(group, dev, None, None), P(group, dev, None)),
        check_vma=False,
    )
```

```python
import jax
import jax.numpy as jnp
from jax import lax
from jax.experimental import pallas as pl
from jax.experimental.pallas import tpu as pltpu
from jax.sharding import Mesh
from jax.sharding import PartitionSpec as P

D = 7168
LAT = 576
LAT_KV = 512
HEAD_V = 128
QK_DIM = 192
EXPERTS = 384
CAP = 2
ROWS = 64
EPSILON = 1e-06
SCALE = QK_DIM ** (-0.5)

NY, NZ, NX = 8, 8, 4
DEVS = NZ * NX
PIECE = 192 // NY
KEYS = 192 * NX
MINE = 2 * ROWS
SENT = MINE + 16
SLOTS = EXPERTS * CAP
OWN_SLOTS = SLOTS // DEVS
BLOCK = 256
BLOCKS = D // BLOCK
TILES = -(-LAT // 128)
PACKED = TILES * MINE + LAT_KV
STEP = 4

bf16 = jnp.bfloat16
f32 = jnp.float32
VMEM = pl.BlockSpec(memory_space=pltpu.VMEM)
SMEM = pl.BlockSpec(memory_space=pltpu.SMEM)


def params():
    return pltpu.CompilerParams(vmem_limit_bytes=24 * 1024 * 1024)


def dot(a, b, dims=((1,), (0,))):
    return lax.dot_general(a, b, (dims, ((), ())), preferred_element_type=f32)


def columns_to_lanes(column):
    return jnp.transpose(jnp.broadcast_to(column, (MINE, 128)))[:1]


def pick_kernel(wanted, mine, other, out):
    core = wanted[8]
    for y in range(NY):
        prompt = wanted[y]
        row = lax.shift_right_logical(prompt, 1)

        @pl.when((prompt & 1) == core)
        def _():
            out[y] = mine[row]

        @pl.when((prompt & 1) != core)
        def _():
            out[y] = other[row]


def pick(wanted, mine, other):
    return pl.pallas_call(
        pick_kernel,
        out_shape=jax.ShapeDtypeStruct(mine.shape, mine.dtype),
        in_specs=[SMEM, VMEM, VMEM],
        out_specs=VMEM,
        compiler_params=params(),
        name="pick",
    )(wanted, mine, other)


def attend(query, keys, visible=None):
    scores = dot(query, keys, ((1,), (1,))) * SCALE
    if visible is not None:
        scores = jnp.where(visible, scores, -1e30)
    best = jnp.max(scores, axis=1, keepdims=True)
    weights = jnp.exp(scores - best)
    total = jnp.sum(weights, axis=1, keepdims=True)
    latent = dot(weights.astype(bf16), keys[:, :LAT_KV]) / total
    return best, total, latent.astype(bf16)


def three(value):
    high = value.astype(bf16).astype(f32)
    rest = value - high
    mid = rest.astype(bf16).astype(f32)
    return high, mid, rest - mid


def pack_kernel(core, query, value_up, out):
    for tile in range(TILES):
        width = min(128, LAT - tile * 128)
        part = query[:, tile * 128 : tile * 128 + width]
        if width < 128:
            part = jnp.concatenate([part, jnp.zeros((MINE, 128 - width), bf16)], axis=1)
        out[tile * MINE : (tile + 1) * MINE, :] = part
    out[TILES * MINE :, :] = value_up[core[0]]


def pack(core, query, value_up):
    return pl.pallas_call(
        pack_kernel,
        out_shape=jax.ShapeDtypeStruct((PACKED, 128), bf16),
        in_specs=[SMEM, VMEM, VMEM],
        out_specs=VMEM,
        compiler_params=params(),
        name="pack",
    )(core, query, value_up)


def attention_kernel(packed, keys, latents, stats):
    index = lax.broadcasted_iota(jnp.int32, (16, 128), 0)
    for step in range(NZ // STEP):
        zs = range(step * STEP, (step + 1) * STEP)
        query = jnp.concatenate(
            [
                jnp.concatenate(
                    [packed[z, tile * MINE : (tile + 1) * MINE, :] for tile in range(TILES)], axis=1
                )
                for z in zs
            ],
            axis=0,
        )[:, :LAT]
        best, total, latent = attend(query, keys[...])
        for i, z in enumerate(zs):
            part = slice(i * MINE, (i + 1) * MINE)
            latents[z] = latent[part]
            rows = three(columns_to_lanes(best[part])) + three(columns_to_lanes(total[part]))
            table = jnp.zeros((16, 128), f32)
            for j, row in enumerate(rows):
                table = jnp.where(index == j, jnp.broadcast_to(row, (16, 128)), table)
            stats[z] = table.astype(bf16)


def prompt_attention(packed, keys):
    return pl.pallas_call(
        attention_kernel,
        out_shape=(
            jax.ShapeDtypeStruct((NZ, MINE, LAT_KV), bf16),
            jax.ShapeDtypeStruct((NZ, 16, 128), bf16),
        ),
        in_specs=[VMEM] * 2,
        out_specs=(VMEM, VMEM),
        compiler_params=params(),
        name="prompt_attention",
    )(packed, keys)


def up_kernel(core, latents, stats, mine, other, out):
    for z in range(NZ):
        out[z, MINE:, :] = stats[z]

    def apply(first, second):
        for z in range(NZ):
            out[z, :ROWS, :] = dot(latents[z, :ROWS], first(z)).astype(bf16)
            out[z, ROWS:MINE, :] = dot(latents[z, ROWS:], second(z)).astype(bf16)

    @pl.when(core[0] == 0)
    def _():
        apply(lambda z: mine[z, TILES * MINE :, :], lambda z: other[z, TILES * MINE :, :])

    @pl.when(core[0] != 0)
    def _():
        apply(lambda z: other[z, TILES * MINE :, :], lambda z: mine[z, TILES * MINE :, :])


def up_project(core, latents, stats, mine, other):
    return pl.pallas_call(
        up_kernel,
        out_shape=jax.ShapeDtypeStruct((NZ, SENT, 128), bf16),
        in_specs=[SMEM] + [VMEM] * 4,
        out_specs=VMEM,
        compiler_params=params(),
        name="up_project",
    )(core, latents, stats, mine, other)


def own_kernel(query, keys, value_up, values, stats):
    row = lax.broadcasted_iota(jnp.int32, (MINE, ROWS), 0) & (ROWS - 1)
    key = lax.broadcasted_iota(jnp.int32, (MINE, ROWS), 1)
    same = lax.shift_right_logical(row, 2) == lax.shift_right_logical(key, 2)
    best, total, latent = attend(query[...], keys[...], same & (key <= row))
    for head in range(2):
        part = slice(head * ROWS, (head + 1) * ROWS)
        values[part, :] = dot(latent[part], value_up[head])
    index = lax.broadcasted_iota(jnp.int32, (8, 128), 0)
    stats[...] = jnp.where(
        index == 0,
        jnp.broadcast_to(columns_to_lanes(best), (8, 128)),
        jnp.broadcast_to(columns_to_lanes(total), (8, 128)),
    )


def own_attention(query, keys, value_up):
    return pl.pallas_call(
        own_kernel,
        out_shape=(
            jax.ShapeDtypeStruct((MINE, HEAD_V), f32),
            jax.ShapeDtypeStruct((8, 128), f32),
        ),
        in_specs=[VMEM] * 3,
        out_specs=(VMEM, VMEM),
        compiler_params=params(),
        name="own_attention",
    )(query, keys, value_up)


def combine_kernel(arrived, own_values, own_stats, out):
    bests, totals = [own_stats[0:1, :]], [own_stats[1:2, :]]
    for z in range(NZ):
        stats = arrived[z, MINE:, :].astype(f32)
        bests.append(stats[0:1] + stats[1:2] + stats[2:3])
        totals.append(stats[3:4] + stats[4:5] + stats[5:6])
    top = bests[0]
    for best in bests[1:]:
        top = jnp.maximum(top, best)
    shares = [total * jnp.exp(best - top) for best, total in zip(bests, totals)]
    whole = shares[0]
    for share in shares[1:]:
        whole = whole + share
    index = lax.broadcasted_iota(jnp.int32, (128, 128), 0)
    table = jnp.zeros((128, 128), f32)
    for i, share in enumerate(shares):
        table = jnp.where(index == i, jnp.broadcast_to(share / whole, (128, 128)), table)
    table = jnp.transpose(table)
    values = table[:, 0:1] * own_values[...]
    for z in range(NZ):
        values = values + table[:, z + 1 : z + 2] * arrived[z, :MINE, :].astype(f32)
    values = values.astype(bf16)
    out[:, :HEAD_V] = values[:ROWS]
    out[:, HEAD_V:] = values[ROWS:]


def combine(arrived, own_values, own_stats):
    return pl.pallas_call(
        combine_kernel,
        out_shape=jax.ShapeDtypeStruct((ROWS, 2 * HEAD_V), bf16),
        in_specs=[VMEM] * 3,
        out_specs=VMEM,
        compiler_params=params(),
        name="combine",
    )(arrived, own_values, own_stats)


def project_kernel(head_values, weight, out):
    for block in range(BLOCKS):
        part = slice(block * BLOCK, (block + 1) * BLOCK)
        out[block] = dot(head_values[...], weight[:, part]).astype(bf16)
    for block in range(BLOCKS, DEVS):
        out[block] = jnp.zeros((ROWS, BLOCK), bf16)


def project(head_values, weight):
    return pl.pallas_call(
        project_kernel,
        out_shape=jax.ShapeDtypeStruct((DEVS, ROWS, BLOCK), bf16),
        in_specs=[VMEM] * 2,
        out_specs=VMEM,
        compiler_params=params(),
        name="project",
    )(head_values, weight)


def slots_kernel(routes, gates, picks, slot_gates):
    slot = lax.broadcasted_iota(jnp.int32, (SLOTS, ROWS), 0)
    expert = lax.shift_right_logical(slot, 1)
    chosen = jnp.zeros((SLOTS, ROWS), f32)
    gating = jnp.zeros((SLOTS, ROWS), f32)
    for k in range(8):
        match = expert == routes[k : k + 1, :]
        chosen = jnp.where(match, 1.0, chosen)
        gating = jnp.where(match, gates[k : k + 1, :], gating)
    earlier = lax.broadcasted_iota(jnp.int32, (ROWS, ROWS), 0) < lax.broadcasted_iota(
        jnp.int32, (ROWS, ROWS), 1
    )
    position = dot(chosen.astype(bf16), jnp.where(earlier, 1.0, 0.0).astype(bf16))
    place = (slot & 1).astype(f32)
    selected = jnp.where(position == place, chosen, 0.0)
    picks[...] = selected.astype(bf16)
    slot_gates[...] = jnp.sum(selected * gating, axis=1, keepdims=True)


def slots(routes, gates):
    return pl.pallas_call(
        slots_kernel,
        out_shape=(
            jax.ShapeDtypeStruct((SLOTS, ROWS), bf16),
            jax.ShapeDtypeStruct((SLOTS, 1), f32),
        ),
        in_specs=[VMEM] * 2,
        out_specs=(VMEM, VMEM),
        compiler_params=params(),
        name="slots",
    )(routes, gates)


def dispatch_kernel(arrived, picks, out):
    total = arrived[0].astype(f32)
    for dev in range(1, DEVS):
        total = total + arrived[dev].astype(f32)
    out[...] = dot(picks[...], total.astype(bf16)).astype(bf16)


def dispatch(arrived, picks):
    return pl.pallas_call(
        dispatch_kernel,
        out_shape=jax.ShapeDtypeStruct((SLOTS, BLOCK), bf16),
        in_specs=[VMEM] * 2,
        out_specs=VMEM,
        compiler_params=params(),
        name="dispatch",
    )(arrived, picks)


def norm_kernel(arrived, gain, out):
    blocks = [arrived[block].astype(f32) for block in range(BLOCKS)]
    square = blocks[0] * blocks[0]
    for block in blocks[1:]:
        square = square + block * block
    scale = lax.rsqrt(jnp.sum(square, axis=1, keepdims=True) * (1.0 / D) + EPSILON)
    for i, block in enumerate(blocks):
        part = slice(i * BLOCK, (i + 1) * BLOCK)
        normed = block * scale * gain[:, part].astype(f32)
        for expert in range(OWN_SLOTS // CAP):
            out[expert, :, part] = normed[expert * CAP : (expert + 1) * CAP]


def norm(arrived, gain):
    return pl.pallas_call(
        norm_kernel,
        out_shape=jax.ShapeDtypeStruct((OWN_SLOTS // CAP, CAP, D), f32),
        in_specs=[VMEM] * 2,
        out_specs=VMEM,
        compiler_params=params(),
        name="norm",
    )(arrived, gain)


def exchange(value, axes):
    return lax.all_to_all(value, axes, split_axis=0, concat_axis=0, tiled=True)


def local(
    prompt_cache,
    prompt_of_group,
    queries,
    new_latents,
    value_up,
    out_weight,
    norm_gain,
    routes,
    gates,
):
    core = lax.axis_index("core")
    dev = lax.axis_index("z") * NX + lax.axis_index("x")

    pieces = exchange(prompt_cache.reshape(NY, PIECE, LAT), "y")
    other = lax.ppermute(pieces, "core", [(0, 1), (1, 0)])
    own_prompts = jnp.where(core == 0, prompt_of_group[0::2], prompt_of_group[1::2])
    wanted = jnp.concatenate([own_prompts, core[None].astype(jnp.int32)])
    served = exchange(pick(wanted, pieces, other), "y").reshape(NY * PIECE, LAT)
    keys = lax.all_gather(served, "x", axis=0, tiled=True)

    query = queries.reshape(ROWS, 2, LAT).transpose(1, 0, 2).reshape(MINE, LAT)
    core = core[None].astype(jnp.int32)
    packed = lax.all_gather(pack(core, query, value_up), "z", axis=0, tiled=True)
    packed = packed.reshape(NZ, PACKED, 128)
    packed, keys = lax.optimization_barrier((packed, keys))
    other_packed = lax.ppermute(packed, "core", [(0, 1), (1, 0)])
    own_values, own_stats = own_attention(query, new_latents.reshape(ROWS, LAT), value_up)
    picks, all_gates = slots(routes.T, gates.T)
    slot_gates = lax.dynamic_slice_in_dim(all_gates, dev * OWN_SLOTS, OWN_SLOTS, 0)

    latents, stats = prompt_attention(packed, keys)
    partial = exchange(up_project(core, latents, stats, packed, other_packed), "z")
    head_values = combine(partial, own_values, own_stats)
    sums = exchange(project(head_values, out_weight), ("z", "x"))
    rows = dispatch(sums, picks).reshape(DEVS, OWN_SLOTS, BLOCK)
    slot_rows = norm(exchange(rows, ("z", "x")), norm_gain.reshape(1, D))
    return (slot_rows[None], slot_gates.reshape(1, OWN_SLOTS // CAP, CAP))


def solution(mesh):
    fine = Mesh(mesh.devices.reshape(NY, 2, NZ, NX), ("y", "core", "z", "x"))
    group, dev = ("y", "core"), ("z", "x")
    return jax.shard_map(
        local,
        mesh=fine,
        in_specs=(
            P(group, dev, None),
            P(),
            P(group, None, None, dev, None),
            P(group, None, None, None),
            P(dev, None, None),
            P(dev, None),
            P(),
            P(group, None),
            P(group, None),
        ),
        out_specs=(P(group, dev, None, None), P(group, dev, None)),
        check_vma=False,
    )
```

```python
import jax
import jax.numpy as jnp
from jax import lax
from jax.experimental import pallas as pl
from jax.experimental.pallas import tpu as pltpu
from jax.sharding import Mesh
from jax.sharding import PartitionSpec as P

D = 7168
LAT = 576
LAT_KV = 512
HEAD_V = 128
QK_DIM = 192
EXPERTS = 384
CAP = 2
ROWS = 64
EPSILON = 1e-06
SCALE = QK_DIM ** (-0.5)

NY, NZ, NX = 8, 8, 4
DEVS = NZ * NX
PIECE = 192 // NY
KEYS = 192 * NX
MINE = 2 * ROWS
SENT = MINE + 16
SLOTS = EXPERTS * CAP
OWN_SLOTS = SLOTS // DEVS
BLOCK = 256
BLOCKS = D // BLOCK
STEP = 4

bf16 = jnp.bfloat16
f32 = jnp.float32
VMEM = pl.BlockSpec(memory_space=pltpu.VMEM)
SMEM = pl.BlockSpec(memory_space=pltpu.SMEM)


def params():
    return pltpu.CompilerParams(vmem_limit_bytes=24 * 1024 * 1024)


def dot(a, b, dims=((1,), (0,))):
    return lax.dot_general(a, b, (dims, ((), ())), preferred_element_type=f32)


def columns_to_lanes(column):
    return jnp.transpose(jnp.broadcast_to(column, (MINE, 128)))[:1]


def pick_kernel(core, prompt_of_group, mine, other, out):
    for y in range(NY):
        prompt = prompt_of_group[2 * y + core[0]]
        row = lax.shift_right_logical(prompt, 1)

        @pl.when((prompt & 1) == core[0])
        def _():
            out[y] = mine[row]

        @pl.when((prompt & 1) != core[0])
        def _():
            out[y] = other[row]


def pick(core, prompt_of_group, mine, other):
    return pl.pallas_call(
        pick_kernel,
        out_shape=jax.ShapeDtypeStruct(mine.shape, mine.dtype),
        in_specs=[SMEM, SMEM, VMEM, VMEM],
        out_specs=VMEM,
        compiler_params=params(),
        name="pick",
    )(core, prompt_of_group, mine, other)


def attend(query, keys, visible=None):
    scores = dot(query, keys, ((1,), (1,))) * SCALE
    if visible is not None:
        scores = jnp.where(visible, scores, -1e30)
    best = jnp.max(scores, axis=1, keepdims=True)
    weights = jnp.exp(scores - best)
    total = jnp.sum(weights, axis=1, keepdims=True)
    latent = dot(weights.astype(bf16), keys[:, :LAT_KV]) / total
    return best, total, latent.astype(bf16)


def three(value):
    high = value.astype(bf16).astype(f32)
    rest = value - high
    mid = rest.astype(bf16).astype(f32)
    return high, mid, rest - mid


def attention_kernel(z, keys, *refs):
    queries, out = refs[:NZ], refs[NZ]
    index = lax.broadcasted_iota(jnp.int32, (16, 128), 0)
    for step in range(NZ // STEP):
        shifts = range(step * STEP, (step + 1) * STEP)
        query = jnp.concatenate([queries[k][...] for k in shifts], axis=0)
        best, total, latent = attend(query, keys[...])
        for i, k in enumerate(shifts):
            part = slice(i * MINE, (i + 1) * MINE)
            owner = (z[0] + NZ - k) & (NZ - 1)
            out[owner, :MINE, :] = latent[part]
            rows = three(columns_to_lanes(best[part])) + three(columns_to_lanes(total[part]))
            table = jnp.zeros((16, 128), f32)
            for j, row in enumerate(rows):
                table = jnp.where(index == j, jnp.broadcast_to(row, (16, 128)), table)
            out[owner, MINE:, :128] = table.astype(bf16)
            out[owner, MINE:, 128:] = jnp.zeros((16, LAT_KV - 128), bf16)


def prompt_attention(z, keys, queries):
    return pl.pallas_call(
        attention_kernel,
        out_shape=jax.ShapeDtypeStruct((NZ, SENT, LAT_KV), bf16),
        in_specs=[SMEM] + [VMEM] * (1 + NZ),
        out_specs=VMEM,
        compiler_params=params(),
        name="prompt_attention",
    )(z, keys, *queries)


def own_kernel(query, keys, latents, stats):
    row = lax.broadcasted_iota(jnp.int32, (MINE, ROWS), 0) & (ROWS - 1)
    key = lax.broadcasted_iota(jnp.int32, (MINE, ROWS), 1)
    same = lax.shift_right_logical(row, 2) == lax.shift_right_logical(key, 2)
    best, total, latent = attend(query[...], keys[...], same & (key <= row))
    latents[...] = latent
    index = lax.broadcasted_iota(jnp.int32, (8, 128), 0)
    stats[...] = jnp.where(
        index == 0,
        jnp.broadcast_to(columns_to_lanes(best), (8, 128)),
        jnp.broadcast_to(columns_to_lanes(total), (8, 128)),
    )


def own_attention(query, keys):
    return pl.pallas_call(
        own_kernel,
        out_shape=(
            jax.ShapeDtypeStruct((MINE, LAT_KV), bf16),
            jax.ShapeDtypeStruct((8, 128), f32),
        ),
        in_specs=[VMEM] * 2,
        out_specs=(VMEM, VMEM),
        compiler_params=params(),
        name="own_attention",
    )(query, keys)


def combine_kernel(arrived, own_latents, own_stats, value_up, out):
    bests, totals = [own_stats[0:1, :]], [own_stats[1:2, :]]
    for z in range(NZ):
        stats = arrived[z, MINE:, :128].astype(f32)
        bests.append(stats[0:1] + stats[1:2] + stats[2:3])
        totals.append(stats[3:4] + stats[4:5] + stats[5:6])
    top = bests[0]
    for best in bests[1:]:
        top = jnp.maximum(top, best)
    shares = [total * jnp.exp(best - top) for best, total in zip(bests, totals)]
    whole = shares[0]
    for share in shares[1:]:
        whole = whole + share
    index = lax.broadcasted_iota(jnp.int32, (128, 128), 0)
    table = jnp.zeros((128, 128), f32)
    for i, share in enumerate(shares):
        table = jnp.where(index == i, jnp.broadcast_to(share / whole, (128, 128)), table)
    table = jnp.transpose(table)
    latent = table[:, 0:1] * own_latents[...].astype(f32)
    for z in range(NZ):
        latent = latent + table[:, z + 1 : z + 2] * arrived[z, :MINE, :].astype(f32)
    latent = latent.astype(bf16)
    for head in range(2):
        values = dot(latent[head * ROWS : (head + 1) * ROWS], value_up[head])
        out[:, head * HEAD_V : (head + 1) * HEAD_V] = values.astype(bf16)


def combine(arrived, own_latents, own_stats, value_up):
    return pl.pallas_call(
        combine_kernel,
        out_shape=jax.ShapeDtypeStruct((ROWS, 2 * HEAD_V), bf16),
        in_specs=[VMEM] * 4,
        out_specs=VMEM,
        compiler_params=params(),
        name="combine",
    )(arrived, own_latents, own_stats, value_up)


def project_kernel(head_values, weight, out):
    for block in range(BLOCKS):
        part = slice(block * BLOCK, (block + 1) * BLOCK)
        out[block] = dot(head_values[...], weight[:, part]).astype(bf16)
    for block in range(BLOCKS, DEVS):
        out[block] = jnp.zeros((ROWS, BLOCK), bf16)


def project(head_values, weight):
    return pl.pallas_call(
        project_kernel,
        out_shape=jax.ShapeDtypeStruct((DEVS, ROWS, BLOCK), bf16),
        in_specs=[VMEM] * 2,
        out_specs=VMEM,
        compiler_params=params(),
        name="project",
    )(head_values, weight)


def slots_kernel(routes, gates, picks, slot_gates):
    slot = lax.broadcasted_iota(jnp.int32, (SLOTS, ROWS), 0)
    expert = lax.shift_right_logical(slot, 1)
    chosen = jnp.zeros((SLOTS, ROWS), f32)
    gating = jnp.zeros((SLOTS, ROWS), f32)
    for k in range(8):
        match = expert == routes[k : k + 1, :]
        chosen = jnp.where(match, 1.0, chosen)
        gating = jnp.where(match, gates[k : k + 1, :], gating)
    earlier = lax.broadcasted_iota(jnp.int32, (ROWS, ROWS), 0) < lax.broadcasted_iota(
        jnp.int32, (ROWS, ROWS), 1
    )
    position = dot(chosen.astype(bf16), jnp.where(earlier, 1.0, 0.0).astype(bf16))
    place = (slot & 1).astype(f32)
    selected = jnp.where(position == place, chosen, 0.0)
    picks[...] = selected.astype(bf16)
    slot_gates[...] = jnp.sum(selected * gating, axis=1, keepdims=True)


def slots(routes, gates):
    return pl.pallas_call(
        slots_kernel,
        out_shape=(
            jax.ShapeDtypeStruct((SLOTS, ROWS), bf16),
            jax.ShapeDtypeStruct((SLOTS, 1), f32),
        ),
        in_specs=[VMEM] * 2,
        out_specs=(VMEM, VMEM),
        compiler_params=params(),
        name="slots",
    )(routes, gates)


def dispatch_kernel(arrived, picks, out):
    total = arrived[0].astype(f32)
    for dev in range(1, DEVS):
        total = total + arrived[dev].astype(f32)
    out[...] = dot(picks[...], total.astype(bf16)).astype(bf16)


def dispatch(arrived, picks):
    return pl.pallas_call(
        dispatch_kernel,
        out_shape=jax.ShapeDtypeStruct((SLOTS, BLOCK), bf16),
        in_specs=[VMEM] * 2,
        out_specs=VMEM,
        compiler_params=params(),
        name="dispatch",
    )(arrived, picks)


def norm_kernel(arrived, gain, out):
    blocks = [arrived[block].astype(f32) for block in range(BLOCKS)]
    square = blocks[0] * blocks[0]
    for block in blocks[1:]:
        square = square + block * block
    scale = lax.rsqrt(jnp.sum(square, axis=1, keepdims=True) * (1.0 / D) + EPSILON)
    for i, block in enumerate(blocks):
        part = slice(i * BLOCK, (i + 1) * BLOCK)
        normed = block * scale * gain[:, part].astype(f32)
        for expert in range(OWN_SLOTS // CAP):
            out[expert, :, part] = normed[expert * CAP : (expert + 1) * CAP]


def norm(arrived, gain):
    return pl.pallas_call(
        norm_kernel,
        out_shape=jax.ShapeDtypeStruct((OWN_SLOTS // CAP, CAP, D), f32),
        in_specs=[VMEM] * 2,
        out_specs=VMEM,
        compiler_params=params(),
        name="norm",
    )(arrived, gain)


def exchange(value, axes):
    return lax.all_to_all(value, axes, split_axis=0, concat_axis=0, tiled=True)


def local(
    prompt_cache,
    prompt_of_group,
    queries,
    new_latents,
    value_up,
    out_weight,
    norm_gain,
    routes,
    gates,
):
    core = lax.axis_index("core")[None].astype(jnp.int32)
    z = lax.axis_index("z")[None].astype(jnp.int32)
    dev = lax.axis_index("z") * NX + lax.axis_index("x")

    query = queries.reshape(ROWS, 2, LAT).transpose(1, 0, 2).reshape(MINE, LAT)

    def shifted(k):
        return lax.ppermute(query, "z", [(i, (i + k) % NZ) for i in range(NZ)])

    pieces = exchange(prompt_cache.reshape(NY, PIECE, LAT), "y")
    near = [1, NZ - 1, 2, NZ - 2]
    pieces, *arrived = lax.optimization_barrier((pieces, *[shifted(k) for k in near]))
    other = lax.ppermute(pieces, "core", [(0, 1), (1, 0)])
    served = exchange(pick(core, prompt_of_group, pieces, other), "y").reshape(NY * PIECE, LAT)
    keys = lax.all_gather(served, "x", axis=0, tiled=True)
    far = [k for k in range(1, NZ) if k not in near]
    by_shift = dict(zip(near + far, arrived + [shifted(k) for k in far]))
    all_queries = [query] + [by_shift[k] for k in range(1, NZ)]
    own_latents, own_stats = own_attention(query, new_latents.reshape(ROWS, LAT))
    picks, all_gates = slots(routes.T, gates.T)
    slot_gates = lax.dynamic_slice_in_dim(all_gates, dev * OWN_SLOTS, OWN_SLOTS, 0)

    partial = exchange(prompt_attention(z, keys, all_queries), "z")
    head_values = combine(partial, own_latents, own_stats, value_up)
    sums = exchange(project(head_values, out_weight), ("z", "x"))
    rows = dispatch(sums, picks).reshape(DEVS, OWN_SLOTS, BLOCK)
    slot_rows = norm(exchange(rows, ("z", "x")), norm_gain.reshape(1, D))
    return (slot_rows[None], slot_gates.reshape(1, OWN_SLOTS // CAP, CAP))


def solution(mesh):
    fine = Mesh(mesh.devices.reshape(NY, 2, NZ, NX), ("y", "core", "z", "x"))
    group, dev = ("y", "core"), ("z", "x")
    return jax.shard_map(
        local,
        mesh=fine,
        in_specs=(
            P(group, dev, None),
            P(),
            P(group, None, None, dev, None),
            P(group, None, None, None),
            P(dev, None, None),
            P(dev, None),
            P(),
            P(group, None),
            P(group, None),
        ),
        out_specs=(P(group, dev, None, None), P(group, dev, None)),
        check_vma=False,
    )
```

```python
import jax
import jax.numpy as jnp
from jax import lax
from jax.experimental import pallas as pl
from jax.experimental.pallas import tpu as pltpu
from jax.sharding import Mesh
from jax.sharding import PartitionSpec as P

D = 7168
LAT = 576
LAT_KV = 512
HEAD_V = 128
QK_DIM = 192
EXPERTS = 384
CAP = 2
ROWS = 64
EPSILON = 1e-06
SCALE = QK_DIM ** (-0.5)

NY, NQ, NL, NX = 8, 4, 2, 4
NEAR = NX * NL
DEVS = NQ * NEAR
PIECE = 192 // NY
KEYS = 192 * NEAR
MINE = 2 * ROWS
SENT = MINE + 16
SLOTS = EXPERTS * CAP
OWN_SLOTS = SLOTS // DEVS
SPAN = D // NEAR
BLOCK = 256
WIDTHS = [min(BLOCK, SPAN - q * BLOCK) for q in range(NQ)]
STEP = 2

bf16 = jnp.bfloat16
f32 = jnp.float32
VMEM = pl.BlockSpec(memory_space=pltpu.VMEM)
SMEM = pl.BlockSpec(memory_space=pltpu.SMEM)


def params():
    return pltpu.CompilerParams(vmem_limit_bytes=24 * 1024 * 1024)


def dot(a, b, dims=((1,), (0,))):
    return lax.dot_general(a, b, (dims, ((), ())), preferred_element_type=f32)


def columns_to_lanes(column):
    return jnp.transpose(jnp.broadcast_to(column, (MINE, 128)))[:1]


def pick_kernel(core, prompt_of_group, mine, other, out):
    for y in range(NY):
        prompt = prompt_of_group[2 * y + core[0]]
        row = lax.shift_right_logical(prompt, 1)

        @pl.when((prompt & 1) == core[0])
        def _():
            out[y] = mine[row]

        @pl.when((prompt & 1) != core[0])
        def _():
            out[y] = other[row]


def pick(core, prompt_of_group, mine, other):
    return pl.pallas_call(
        pick_kernel,
        out_shape=jax.ShapeDtypeStruct(mine.shape, mine.dtype),
        in_specs=[SMEM, SMEM, VMEM, VMEM],
        out_specs=VMEM,
        compiler_params=params(),
        name="pick",
    )(core, prompt_of_group, mine, other)


def attend(query, keys, visible=None):
    scores = dot(query, keys, ((1,), (1,))) * SCALE
    if visible is not None:
        scores = jnp.where(visible, scores, -1e30)
    best = jnp.max(scores, axis=1, keepdims=True)
    weights = jnp.exp(scores - best)
    total = jnp.sum(weights, axis=1, keepdims=True)
    latent = dot(weights.astype(bf16), keys[:, :LAT_KV]) / total
    return best, total, latent.astype(bf16)


def three(value):
    high = value.astype(bf16).astype(f32)
    rest = value - high
    mid = rest.astype(bf16).astype(f32)
    return high, mid, rest - mid


def attention_kernel(zq, keys, *refs):
    queries, out = refs[:NQ], refs[NQ]
    index = lax.broadcasted_iota(jnp.int32, (16, 128), 0)
    for step in range(NQ // STEP):
        shifts = range(step * STEP, (step + 1) * STEP)
        query = jnp.concatenate([queries[k][...] for k in shifts], axis=0)
        best, total, latent = attend(query, keys[...])
        for i, k in enumerate(shifts):
            part = slice(i * MINE, (i + 1) * MINE)
            owner = (zq[0] + NQ - k) & (NQ - 1)
            out[owner, :MINE, :] = latent[part]
            rows = three(columns_to_lanes(best[part])) + three(columns_to_lanes(total[part]))
            table = jnp.zeros((16, 128), f32)
            for j, row in enumerate(rows):
                table = jnp.where(index == j, jnp.broadcast_to(row, (16, 128)), table)
            out[owner, MINE:, :128] = table.astype(bf16)
            out[owner, MINE:, 128:] = jnp.zeros((16, LAT_KV - 128), bf16)


def prompt_attention(zq, keys, queries):
    return pl.pallas_call(
        attention_kernel,
        out_shape=jax.ShapeDtypeStruct((NQ, SENT, LAT_KV), bf16),
        in_specs=[SMEM] + [VMEM] * (1 + NQ),
        out_specs=VMEM,
        compiler_params=params(),
        name="prompt_attention",
    )(zq, keys, *queries)


def own_kernel(query, keys, latents, stats):
    row = lax.broadcasted_iota(jnp.int32, (MINE, ROWS), 0) & (ROWS - 1)
    key = lax.broadcasted_iota(jnp.int32, (MINE, ROWS), 1)
    same = lax.shift_right_logical(row, 2) == lax.shift_right_logical(key, 2)
    best, total, latent = attend(query[...], keys[...], same & (key <= row))
    latents[...] = latent
    index = lax.broadcasted_iota(jnp.int32, (8, 128), 0)
    stats[...] = jnp.where(
        index == 0,
        jnp.broadcast_to(columns_to_lanes(best), (8, 128)),
        jnp.broadcast_to(columns_to_lanes(total), (8, 128)),
    )


def own_attention(query, keys):
    return pl.pallas_call(
        own_kernel,
        out_shape=(
            jax.ShapeDtypeStruct((MINE, LAT_KV), bf16),
            jax.ShapeDtypeStruct((8, 128), f32),
        ),
        in_specs=[VMEM] * 2,
        out_specs=(VMEM, VMEM),
        compiler_params=params(),
        name="own_attention",
    )(query, keys)


def combine_kernel(arrived, own_latents, own_stats, value_up, out):
    bests, totals = [own_stats[0:1, :]], [own_stats[1:2, :]]
    for z in range(NQ):
        stats = arrived[z, MINE:, :128].astype(f32)
        bests.append(stats[0:1] + stats[1:2] + stats[2:3])
        totals.append(stats[3:4] + stats[4:5] + stats[5:6])
    top = bests[0]
    for best in bests[1:]:
        top = jnp.maximum(top, best)
    shares = [total * jnp.exp(best - top) for best, total in zip(bests, totals)]
    whole = shares[0]
    for share in shares[1:]:
        whole = whole + share
    index = lax.broadcasted_iota(jnp.int32, (128, 128), 0)
    table = jnp.zeros((128, 128), f32)
    for i, share in enumerate(shares):
        table = jnp.where(index == i, jnp.broadcast_to(share / whole, (128, 128)), table)
    table = jnp.transpose(table)
    latent = table[:, 0:1] * own_latents[...].astype(f32)
    for z in range(NQ):
        latent = latent + table[:, z + 1 : z + 2] * arrived[z, :MINE, :].astype(f32)
    latent = latent.astype(bf16)
    for head in range(2):
        values = dot(latent[head * ROWS : (head + 1) * ROWS], value_up[head])
        out[:, head * HEAD_V : (head + 1) * HEAD_V] = values.astype(bf16)


def combine(arrived, own_latents, own_stats, value_up):
    return pl.pallas_call(
        combine_kernel,
        out_shape=jax.ShapeDtypeStruct((ROWS, 2 * HEAD_V), bf16),
        in_specs=[VMEM] * 4,
        out_specs=VMEM,
        compiler_params=params(),
        name="combine",
    )(arrived, own_latents, own_stats, value_up)


def project_kernel(head_values, weight, out, held, sems):
    copies = [
        pltpu.make_async_copy(weight.at[:, i * SPAN : (i + 1) * SPAN], held.at[i], sems.at[i])
        for i in range(NEAR)
    ]
    for copy in copies:
        copy.start()
    for i, copy in enumerate(copies):
        copy.wait()
        out[i] = dot(head_values[...], held[i]).astype(bf16)


def project(head_values, weight):
    return pl.pallas_call(
        project_kernel,
        out_shape=jax.ShapeDtypeStruct((NEAR, ROWS, SPAN), bf16),
        in_specs=[VMEM, pl.BlockSpec(memory_space=pltpu.HBM)],
        out_specs=VMEM,
        scratch_shapes=[
            pltpu.VMEM((NEAR, 2 * HEAD_V, SPAN), bf16),
            pltpu.SemaphoreType.DMA((NEAR,)),
        ],
        compiler_params=params(),
        name="project",
    )(head_values, weight)


def add_kernel(arrived, out):
    total = arrived[0].astype(f32)
    for i in range(1, NEAR):
        total = total + arrived[i].astype(f32)
    total = total.astype(bf16)
    for q, width in enumerate(WIDTHS):
        out[q, :, :width] = total[:, q * BLOCK : q * BLOCK + width]
        if width < BLOCK:
            out[q, :, width:] = jnp.zeros((ROWS, BLOCK - width), bf16)


def add(arrived):
    return pl.pallas_call(
        add_kernel,
        out_shape=jax.ShapeDtypeStruct((NQ, ROWS, BLOCK), bf16),
        in_specs=[VMEM],
        out_specs=VMEM,
        compiler_params=params(),
        name="add",
    )(arrived)


def slots_kernel(routes, gates, picks, slot_gates):
    slot = lax.broadcasted_iota(jnp.int32, (SLOTS, ROWS), 0)
    expert = lax.shift_right_logical(slot, 1)
    chosen = jnp.zeros((SLOTS, ROWS), f32)
    gating = jnp.zeros((SLOTS, ROWS), f32)
    for k in range(8):
        match = expert == routes[k : k + 1, :]
        chosen = jnp.where(match, 1.0, chosen)
        gating = jnp.where(match, gates[k : k + 1, :], gating)
    earlier = lax.broadcasted_iota(jnp.int32, (ROWS, ROWS), 0) < lax.broadcasted_iota(
        jnp.int32, (ROWS, ROWS), 1
    )
    position = dot(chosen.astype(bf16), jnp.where(earlier, 1.0, 0.0).astype(bf16))
    place = (slot & 1).astype(f32)
    selected = jnp.where(position == place, chosen, 0.0)
    picks[...] = selected.astype(bf16)
    slot_gates[...] = jnp.sum(selected * gating, axis=1, keepdims=True)


def slots(routes, gates):
    return pl.pallas_call(
        slots_kernel,
        out_shape=(
            jax.ShapeDtypeStruct((SLOTS, ROWS), bf16),
            jax.ShapeDtypeStruct((SLOTS, 1), f32),
        ),
        in_specs=[VMEM] * 2,
        out_specs=(VMEM, VMEM),
        compiler_params=params(),
        name="slots",
    )(routes, gates)


def dispatch_kernel(arrived, picks, out):
    total = arrived[0].astype(f32)
    for q in range(1, NQ):
        total = total + arrived[q].astype(f32)
    out[...] = dot(picks[...], total.astype(bf16)).astype(bf16)


def dispatch(arrived, picks):
    return pl.pallas_call(
        dispatch_kernel,
        out_shape=jax.ShapeDtypeStruct((SLOTS, BLOCK), bf16),
        in_specs=[VMEM] * 2,
        out_specs=VMEM,
        compiler_params=params(),
        name="dispatch",
    )(arrived, picks)


def norm_kernel(arrived, gain, out):
    blocks = []
    for x in range(NX):
        for zl in range(NL):
            for q, width in enumerate(WIDTHS):
                block = arrived[(q * NL + zl) * NX + x]
                blocks.append(block[:, :width].astype(f32))
    square = jnp.zeros((OWN_SLOTS, 128), f32)
    for block in blocks:
        for lane in range(0, block.shape[1], 128):
            part = block[:, lane : lane + 128]
            square = square + part * part
    scale = lax.rsqrt(jnp.sum(square, axis=1, keepdims=True) * (1.0 / D) + EPSILON)
    start = 0
    for block in blocks:
        part = slice(start, start + block.shape[1])
        start = start + block.shape[1]
        normed = block * scale * gain[:, part].astype(f32)
        for expert in range(OWN_SLOTS // CAP):
            out[expert, :, part] = normed[expert * CAP : (expert + 1) * CAP]


def norm(arrived, gain):
    return pl.pallas_call(
        norm_kernel,
        out_shape=jax.ShapeDtypeStruct((OWN_SLOTS // CAP, CAP, D), f32),
        in_specs=[VMEM] * 2,
        out_specs=VMEM,
        compiler_params=params(),
        name="norm",
    )(arrived, gain)


def exchange(value, axes):
    return lax.all_to_all(value, axes, split_axis=0, concat_axis=0, tiled=True)


def local(
    prompt_cache,
    prompt_of_group,
    queries,
    new_latents,
    value_up,
    out_weight,
    norm_gain,
    routes,
    gates,
):
    core = lax.axis_index("core")[None].astype(jnp.int32)
    zq = lax.axis_index("zq")[None].astype(jnp.int32)
    dev = (lax.axis_index("zq") * NL + lax.axis_index("zl")) * NX + lax.axis_index("x")

    query = queries.reshape(ROWS, 2, LAT).transpose(1, 0, 2).reshape(MINE, LAT)

    def shifted(k):
        return lax.ppermute(query, "zq", [(i, (i + k) % NQ) for i in range(NQ)])

    pieces = exchange(prompt_cache.reshape(NY, PIECE, LAT), "y")
    pieces, one, three_ = lax.optimization_barrier((pieces, shifted(1), shifted(3)))
    other = lax.ppermute(pieces, "core", [(0, 1), (1, 0)])
    served = exchange(pick(core, prompt_of_group, pieces, other), "y").reshape(NY * PIECE, LAT)
    served, two = lax.optimization_barrier((served, shifted(2)))
    keys = exchange(jnp.broadcast_to(served, (NEAR, NY * PIECE, LAT)), ("x", "zl"))
    keys = keys.reshape(KEYS, LAT)
    all_queries = [query, one, two, three_]
    own_latents, own_stats = own_attention(query, new_latents.reshape(ROWS, LAT))
    picks, all_gates = slots(routes.T, gates.T)
    slot_gates = lax.dynamic_slice_in_dim(all_gates, dev * OWN_SLOTS, OWN_SLOTS, 0)

    partial = exchange(prompt_attention(zq, keys, all_queries), "zq")
    head_values = combine(partial, own_latents, own_stats, value_up)
    sums = exchange(add(exchange(project(head_values, out_weight), ("x", "zl"))), "zq")
    rows = dispatch(sums, picks).reshape(DEVS, OWN_SLOTS, BLOCK)
    slot_rows = norm(exchange(rows, ("zq", "zl", "x")), norm_gain.reshape(1, D))
    return (slot_rows[None], slot_gates.reshape(1, OWN_SLOTS // CAP, CAP))


def solution(mesh):
    axes = ("y", "core", "zq", "zl", "x")
    fine = Mesh(mesh.devices.reshape(NY, 2, NQ, NL, NX), axes)
    group, dev = axes[:2], axes[2:]
    return jax.shard_map(
        local,
        mesh=fine,
        in_specs=(
            P(group, dev, None),
            P(),
            P(group, None, None, dev, None),
            P(group, None, None, None),
            P(dev, None, None),
            P(dev, None),
            P(),
            P(group, None),
            P(group, None),
        ),
        out_specs=(P(group, dev, None, None), P(group, dev, None)),
        check_vma=False,
    )
```

```python
import jax
import jax.numpy as jnp
from jax import lax
from jax.experimental import pallas as pl
from jax.experimental.pallas import tpu as pltpu
from jax.sharding import Mesh
from jax.sharding import PartitionSpec as P

D = 7168
LAT = 576
LAT_KV = 512
HEAD_V = 128
QK_DIM = 192
EXPERTS = 384
CAP = 2
ROWS = 64
EPSILON = 1e-06
SCALE = QK_DIM ** (-0.5)

NY, NQ, NL, NX = 8, 4, 2, 4
NZ = NQ * NL
NEAR = NL * NX
DEVS = NQ * NEAR
PIECE = 192 // NY
KEYS = 192 * NX
MINE = 2 * ROWS
SENT = MINE + 16
SLOTS = EXPERTS * CAP
OWN_SLOTS = SLOTS // DEVS
NEAR_SLOTS = NEAR * OWN_SLOTS
SPAN = D // NEAR
UP_AT = LAT_KV // 128 * MINE + ROWS
PACKED = UP_AT + LAT_KV
STEP = 4

bf16 = jnp.bfloat16
f32 = jnp.float32
VMEM = pl.BlockSpec(memory_space=pltpu.VMEM)
SMEM = pl.BlockSpec(memory_space=pltpu.SMEM)


def params(mib=24):
    return pltpu.CompilerParams(vmem_limit_bytes=mib * 1024 * 1024)


def dot(a, b, dims=((1,), (0,))):
    return lax.dot_general(a, b, (dims, ((), ())), preferred_element_type=f32)


def columns_to_lanes(column):
    return jnp.transpose(jnp.broadcast_to(column, (MINE, 128)))[:1]


def pick_kernel(core, wanted, mine, other, out):
    for y in range(NY):
        prompt = wanted[y]
        row = lax.shift_right_logical(prompt, 1)

        @pl.when((prompt & 1) == core[0])
        def _():
            out[y] = mine[row]

        @pl.when((prompt & 1) != core[0])
        def _():
            out[y] = other[row]


def pick(core, wanted, mine, other):
    return pl.pallas_call(
        pick_kernel,
        out_shape=jax.ShapeDtypeStruct(mine.shape, mine.dtype),
        in_specs=[SMEM, SMEM, VMEM, VMEM],
        out_specs=VMEM,
        compiler_params=params(),
        name="pick",
    )(core, wanted, mine, other)


def attend(query, keys, visible=None):
    scores = dot(query, keys, ((1,), (1,))) * SCALE
    if visible is not None:
        scores = jnp.where(visible, scores, -1e30)
    best = jnp.max(scores, axis=1, keepdims=True)
    weights = jnp.exp(scores - best)
    total = jnp.sum(weights, axis=1, keepdims=True)
    latent = dot(weights.astype(bf16), keys[:, :LAT_KV]) / total
    return best, total, latent.astype(bf16)


def three(value):
    high = value.astype(bf16).astype(f32)
    rest = value - high
    mid = rest.astype(bf16).astype(f32)
    return high, mid, rest - mid


def pack_kernel(core, query, value_up, out, sem):
    copy = pltpu.make_async_copy(value_up.at[core[0]], out.at[UP_AT:], sem)
    copy.start()
    heads = [query[:, head, :] for head in range(2)]
    for tile in range(LAT_KV // 128):
        for head in range(2):
            first = tile * MINE + head * ROWS
            out[first : first + ROWS, :] = heads[head][:, tile * 128 : (tile + 1) * 128]
    out[UP_AT - ROWS : UP_AT, :] = jnp.concatenate([head[:, LAT_KV:] for head in heads], axis=1)
    copy.wait()


def pack(core, query, value_up):
    return pl.pallas_call(
        pack_kernel,
        out_shape=jax.ShapeDtypeStruct((PACKED, 128), bf16),
        in_specs=[SMEM, VMEM, pl.BlockSpec(memory_space=pl.ANY)],
        out_specs=VMEM,
        scratch_shapes=[pltpu.SemaphoreType.DMA],
        compiler_params=params(60),
        name="pack",
    )(core, query, value_up)


def unpacked(packed, z):
    tiles = [packed[z, tile * MINE : (tile + 1) * MINE, :] for tile in range(LAT_KV // 128)]
    rest = packed[z, UP_AT - ROWS : UP_AT, :]
    width = LAT - LAT_KV
    tiles.append(jnp.concatenate([rest[:, :width], rest[:, width:]], axis=0))
    return jnp.concatenate(tiles, axis=1)


def attention_kernel(packed, keys, latents, stats):
    index = lax.broadcasted_iota(jnp.int32, (16, 128), 0)
    for step in range(NZ // STEP):
        zs = range(step * STEP, (step + 1) * STEP)
        query = jnp.concatenate([unpacked(packed, z) for z in zs], axis=0)
        best, total, latent = attend(query, keys[...])
        for i, z in enumerate(zs):
            part = slice(i * MINE, (i + 1) * MINE)
            latents[z] = latent[part]
            rows = three(columns_to_lanes(best[part])) + three(columns_to_lanes(total[part]))
            table = jnp.zeros((16, 128), f32)
            for j, row in enumerate(rows):
                table = jnp.where(index == j, jnp.broadcast_to(row, (16, 128)), table)
            stats[z] = table.astype(bf16)


def prompt_attention(packed, keys):
    return pl.pallas_call(
        attention_kernel,
        out_shape=(
            jax.ShapeDtypeStruct((NZ, MINE, LAT_KV), bf16),
            jax.ShapeDtypeStruct((NZ, 16, 128), bf16),
        ),
        in_specs=[VMEM] * 2,
        out_specs=(VMEM, VMEM),
        compiler_params=params(),
        name="prompt_attention",
    )(packed, keys)


def up_kernel(core, latents, stats, mine, other, out):
    for z in range(NZ):
        out[z, MINE:, :] = stats[z]

    def apply(first, second):
        for z in range(NZ):
            out[z, :ROWS, :] = dot(latents[z, :ROWS], first(z)).astype(bf16)
            out[z, ROWS:MINE, :] = dot(latents[z, ROWS:], second(z)).astype(bf16)

    @pl.when(core[0] == 0)
    def _():
        apply(lambda z: mine[z, UP_AT:, :], lambda z: other[z, UP_AT:, :])

    @pl.when(core[0] != 0)
    def _():
        apply(lambda z: other[z, UP_AT:, :], lambda z: mine[z, UP_AT:, :])


def up_project(core, latents, stats, mine, other):
    return pl.pallas_call(
        up_kernel,
        out_shape=jax.ShapeDtypeStruct((NZ, SENT, 128), bf16),
        in_specs=[SMEM] + [VMEM] * 4,
        out_specs=VMEM,
        compiler_params=params(),
        name="up_project",
    )(core, latents, stats, mine, other)


def own_kernel(query, keys, value_up, values, stats):
    row = lax.broadcasted_iota(jnp.int32, (MINE, ROWS), 0) & (ROWS - 1)
    key = lax.broadcasted_iota(jnp.int32, (MINE, ROWS), 1)
    same = lax.shift_right_logical(row, 2) == lax.shift_right_logical(key, 2)
    best, total, latent = attend(query[...], keys[...], same & (key <= row))
    for head in range(2):
        part = slice(head * ROWS, (head + 1) * ROWS)
        values[part, :] = dot(latent[part], value_up[head])
    index = lax.broadcasted_iota(jnp.int32, (8, 128), 0)
    stats[...] = jnp.where(
        index == 0,
        jnp.broadcast_to(columns_to_lanes(best), (8, 128)),
        jnp.broadcast_to(columns_to_lanes(total), (8, 128)),
    )


def own_attention(query, keys, value_up):
    return pl.pallas_call(
        own_kernel,
        out_shape=(
            jax.ShapeDtypeStruct((MINE, HEAD_V), f32),
            jax.ShapeDtypeStruct((8, 128), f32),
        ),
        in_specs=[VMEM] * 3,
        out_specs=(VMEM, VMEM),
        compiler_params=params(),
        name="own_attention",
    )(query, keys, value_up)


def combine_kernel(arrived, own_values, own_stats, out):
    bests, totals = [own_stats[0:1, :]], [own_stats[1:2, :]]
    for z in range(NZ):
        stats = arrived[z, MINE:, :].astype(f32)
        bests.append(stats[0:1] + stats[1:2] + stats[2:3])
        totals.append(stats[3:4] + stats[4:5] + stats[5:6])
    top = bests[0]
    for best in bests[1:]:
        top = jnp.maximum(top, best)
    shares = [total * jnp.exp(best - top) for best, total in zip(bests, totals)]
    whole = shares[0]
    for share in shares[1:]:
        whole = whole + share
    index = lax.broadcasted_iota(jnp.int32, (128, 128), 0)
    table = jnp.zeros((128, 128), f32)
    for i, share in enumerate(shares):
        table = jnp.where(index == i, jnp.broadcast_to(share / whole, (128, 128)), table)
    table = jnp.transpose(table)
    values = table[:, 0:1] * own_values[...]
    for z in range(NZ):
        values = values + table[:, z + 1 : z + 2] * arrived[z, :MINE, :].astype(f32)
    values = values.astype(bf16)
    out[:, :HEAD_V] = values[:ROWS]
    out[:, HEAD_V:] = values[ROWS:]


def combine(arrived, own_values, own_stats):
    return pl.pallas_call(
        combine_kernel,
        out_shape=jax.ShapeDtypeStruct((ROWS, 2 * HEAD_V), bf16),
        in_specs=[VMEM] * 3,
        out_specs=VMEM,
        compiler_params=params(),
        name="combine",
    )(arrived, own_values, own_stats)


def project_kernel(head_values, weight, out):
    for i in range(NEAR):
        out[i] = dot(head_values[...], weight[:, i * SPAN : (i + 1) * SPAN]).astype(bf16)


def project(head_values, weight):
    return pl.pallas_call(
        project_kernel,
        out_shape=jax.ShapeDtypeStruct((NEAR, ROWS, SPAN), bf16),
        in_specs=[VMEM] * 2,
        out_specs=VMEM,
        compiler_params=params(),
        name="project",
    )(head_values, weight)


def add_kernel(arrived, out):
    total = arrived[0].astype(f32)
    for i in range(1, NEAR):
        total = total + arrived[i].astype(f32)
    total = total.astype(bf16)
    for q in range(NQ):
        out[q] = total


def add(arrived):
    return pl.pallas_call(
        add_kernel,
        out_shape=jax.ShapeDtypeStruct((NQ, ROWS, SPAN), bf16),
        in_specs=[VMEM],
        out_specs=VMEM,
        compiler_params=params(),
        name="add",
    )(arrived)


def slots_kernel(routes, gates, picks, slot_gates):
    slot = lax.broadcasted_iota(jnp.int32, (SLOTS, ROWS), 0)
    expert = lax.shift_right_logical(slot, 1)
    chosen = jnp.zeros((SLOTS, ROWS), f32)
    gating = jnp.zeros((SLOTS, ROWS), f32)
    for k in range(8):
        match = expert == routes[k : k + 1, :]
        chosen = jnp.where(match, 1.0, chosen)
        gating = jnp.where(match, gates[k : k + 1, :], gating)
    earlier = lax.broadcasted_iota(jnp.int32, (ROWS, ROWS), 0) < lax.broadcasted_iota(
        jnp.int32, (ROWS, ROWS), 1
    )
    position = dot(chosen.astype(bf16), jnp.where(earlier, 1.0, 0.0).astype(bf16))
    place = (slot & 1).astype(f32)
    selected = jnp.where(position == place, chosen, 0.0)
    picks[...] = selected.astype(bf16)
    slot_gates[...] = jnp.sum(selected * gating, axis=1, keepdims=True)


def slots(routes, gates):
    return pl.pallas_call(
        slots_kernel,
        out_shape=(
            jax.ShapeDtypeStruct((SLOTS, ROWS), bf16),
            jax.ShapeDtypeStruct((SLOTS, 1), f32),
        ),
        in_specs=[VMEM] * 2,
        out_specs=(VMEM, VMEM),
        compiler_params=params(),
        name="slots",
    )(routes, gates)


def dispatch_kernel(zq, arrived, picks, out):
    total = arrived[0].astype(f32)
    for q in range(1, NQ):
        total = total + arrived[q].astype(f32)
    first = pl.multiple_of(zq[0] * NEAR_SLOTS, NEAR_SLOTS)
    out[...] = dot(picks[pl.ds(first, NEAR_SLOTS), :], total.astype(bf16)).astype(bf16)


def dispatch(zq, arrived, picks):
    return pl.pallas_call(
        dispatch_kernel,
        out_shape=jax.ShapeDtypeStruct((NEAR_SLOTS, SPAN), bf16),
        in_specs=[SMEM, VMEM, VMEM],
        out_specs=VMEM,
        compiler_params=params(),
        name="dispatch",
    )(zq, arrived, picks)


def norm_kernel(arrived, gain, out):
    square = jnp.zeros((OWN_SLOTS, 128), f32)
    for i in range(NEAR):
        block = arrived[i].astype(f32)
        for lane in range(0, SPAN, 128):
            part = block[:, lane : lane + 128]
            square = square + part * part
    scale = lax.rsqrt(jnp.sum(square, axis=1, keepdims=True) * (1.0 / D) + EPSILON)
    for i in range(NEAR):
        part = slice(i * SPAN, (i + 1) * SPAN)
        normed = arrived[i].astype(f32) * scale * gain[:, part].astype(f32)
        for expert in range(OWN_SLOTS // CAP):
            out[expert, :, part] = normed[expert * CAP : (expert + 1) * CAP]


def norm(arrived, gain):
    return pl.pallas_call(
        norm_kernel,
        out_shape=jax.ShapeDtypeStruct((OWN_SLOTS // CAP, CAP, D), f32),
        in_specs=[VMEM] * 2,
        out_specs=VMEM,
        compiler_params=params(),
        name="norm",
    )(arrived, gain)


def exchange(value, axes):
    return lax.all_to_all(value, axes, split_axis=0, concat_axis=0, tiled=True)


def local(
    prompt_cache,
    prompt_of_group,
    queries,
    new_latents,
    value_up,
    out_weight,
    norm_gain,
    routes,
    gates,
):
    core = lax.axis_index("core")[None].astype(jnp.int32)
    zq = lax.axis_index("zq")[None].astype(jnp.int32)
    dev = (lax.axis_index("zq") * NL + lax.axis_index("zl")) * NX + lax.axis_index("x")
    swap = [(0, 1), (1, 0)]

    pieces = exchange(prompt_cache.reshape(NY, PIECE, LAT), "y")
    other = lax.ppermute(pieces, "core", swap)
    wanted = jnp.where(core[0] == 0, prompt_of_group[0::2], prompt_of_group[1::2])
    served = exchange(pick(core, wanted, pieces, other), "y").reshape(NY * PIECE, LAT)
    keys = lax.all_gather(served, "x", axis=0, tiled=True)

    query = queries.reshape(ROWS, 2, LAT).transpose(1, 0, 2).reshape(MINE, LAT)
    packed = lax.all_gather(pack(core, queries.reshape(ROWS, 2, LAT), value_up), ("zq", "zl"), axis=0, tiled=True)
    packed = packed.reshape(NZ, PACKED, 128)
    packed, keys = lax.optimization_barrier((packed, keys))
    other_packed = lax.ppermute(packed, "core", swap)
    picks, all_gates = slots(routes.T, gates.T)
    slot_gates = lax.dynamic_slice_in_dim(all_gates, dev * OWN_SLOTS, OWN_SLOTS, 0)

    latents, stats = prompt_attention(packed, keys)
    values = up_project(core, latents, stats, packed, other_packed)
    own_values, own_stats = own_attention(query, new_latents.reshape(ROWS, LAT), value_up)
    partial = exchange(values, ("zq", "zl"))
    head_values = combine(partial, own_values, own_stats)
    sums = exchange(add(exchange(project(head_values, out_weight), ("zl", "x"))), "zq")
    rows = dispatch(zq, sums, picks).reshape(NEAR, OWN_SLOTS, SPAN)
    slot_rows = norm(exchange(rows, ("zl", "x")), norm_gain.reshape(1, D))
    return (slot_rows[None], slot_gates.reshape(1, OWN_SLOTS // CAP, CAP))


def solution(mesh):
    axes = ("y", "core", "zq", "zl", "x")
    fine = Mesh(mesh.devices.reshape(NY, 2, NQ, NL, NX), axes)
    group, dev = axes[:2], axes[2:]
    return jax.shard_map(
        local,
        mesh=fine,
        in_specs=(
            P(group, dev, None),
            P(),
            P(group, None, None, dev, None),
            P(group, None, None, None),
            P(dev, None, None),
            P(dev, None),
            P(),
            P(group, None),
            P(group, None),
        ),
        out_specs=(P(group, dev, None, None), P(group, dev, None)),
        check_vma=False,
    )
```

```python
import jax
import jax.numpy as jnp
from jax import lax
from jax.experimental import pallas as pl
from jax.experimental.pallas import tpu as pltpu
from jax.sharding import Mesh
from jax.sharding import PartitionSpec as P

D = 7168
LAT = 576
LAT_KV = 512
HEAD_V = 128
QK_DIM = 192
EXPERTS = 384
CAP = 2
ROWS = 64
EPSILON = 1e-06
SCALE = QK_DIM ** (-0.5)

NY, NQ, NL, NX = 8, 4, 2, 4
NEAR = NL * NX
DEVS = NQ * NEAR
PIECE = 192 // NY
KEYS = 192 * NQ
MINE = 2 * ROWS
SENT = MINE + 16
SLOTS = EXPERTS * CAP
OWN_SLOTS = SLOTS // DEVS
NEAR_SLOTS = NEAR * OWN_SLOTS
SPAN = D // NEAR

bf16 = jnp.bfloat16
f32 = jnp.float32
VMEM = pl.BlockSpec(memory_space=pltpu.VMEM)
SMEM = pl.BlockSpec(memory_space=pltpu.SMEM)


def params(mib=24):
    return pltpu.CompilerParams(vmem_limit_bytes=mib * 1024 * 1024)


def dot(a, b, dims=((1,), (0,))):
    return lax.dot_general(a, b, (dims, ((), ())), preferred_element_type=f32)


def columns_to_lanes(column):
    return jnp.transpose(jnp.broadcast_to(column, (MINE, 128)))[:1]


def pick_kernel(core, wanted, mine, other, out):
    for y in range(NY):
        prompt = wanted[y]
        row = lax.shift_right_logical(prompt, 1)

        @pl.when((prompt & 1) == core[0])
        def _():
            out[y] = mine[row]

        @pl.when((prompt & 1) != core[0])
        def _():
            out[y] = other[row]


def pick(core, wanted, mine, other):
    return pl.pallas_call(
        pick_kernel,
        out_shape=jax.ShapeDtypeStruct(mine.shape, mine.dtype),
        in_specs=[SMEM, SMEM, VMEM, VMEM],
        out_specs=VMEM,
        compiler_params=params(),
        name="pick",
    )(core, wanted, mine, other)


def attend(query, keys, visible=None):
    scores = dot(query, keys, ((1,), (1,))) * SCALE
    if visible is not None:
        scores = jnp.where(visible, scores, -1e30)
    best = jnp.max(scores, axis=1, keepdims=True)
    weights = jnp.exp(scores - best)
    total = jnp.sum(weights, axis=1, keepdims=True)
    latent = dot(weights.astype(bf16), keys[:, :LAT_KV]) / total
    return best, total, latent.astype(bf16)


def three(value):
    high = value.astype(bf16).astype(f32)
    rest = value - high
    mid = rest.astype(bf16).astype(f32)
    return high, mid, rest - mid


def attention_kernel(zl, mine, other, keys, out):
    index = lax.broadcasted_iota(jnp.int32, (16, 128), 0)
    for step in range(NL):
        queries = (mine, other)[step]
        first = (zl[0] ^ step) * NX
        query = jnp.concatenate([queries[x] for x in range(NX)], axis=0)
        best, total, latent = attend(query, keys[...])
        for i in range(NX):
            part = slice(i * MINE, (i + 1) * MINE)
            owner = first + i
            out[owner, :MINE, :] = latent[part]
            rows = three(columns_to_lanes(best[part])) + three(columns_to_lanes(total[part]))
            table = jnp.zeros((16, 128), f32)
            for j, row in enumerate(rows):
                table = jnp.where(index == j, jnp.broadcast_to(row, (16, 128)), table)
            out[owner, MINE:, :128] = table.astype(bf16)
            out[owner, MINE:, 128:] = jnp.zeros((16, LAT_KV - 128), bf16)


def prompt_attention(zl, mine, other, keys):
    return pl.pallas_call(
        attention_kernel,
        out_shape=jax.ShapeDtypeStruct((NEAR, SENT, LAT_KV), bf16),
        in_specs=[SMEM] + [VMEM] * 3,
        out_specs=VMEM,
        compiler_params=params(),
        name="prompt_attention",
    )(zl, mine, other, keys)


def own_kernel(query, keys, latents, stats):
    row = lax.broadcasted_iota(jnp.int32, (MINE, ROWS), 0) & (ROWS - 1)
    key = lax.broadcasted_iota(jnp.int32, (MINE, ROWS), 1)
    same = lax.shift_right_logical(row, 2) == lax.shift_right_logical(key, 2)
    best, total, latent = attend(query[...], keys[...], same & (key <= row))
    latents[...] = latent
    index = lax.broadcasted_iota(jnp.int32, (8, 128), 0)
    stats[...] = jnp.where(
        index == 0,
        jnp.broadcast_to(columns_to_lanes(best), (8, 128)),
        jnp.broadcast_to(columns_to_lanes(total), (8, 128)),
    )


def own_attention(query, keys):
    return pl.pallas_call(
        own_kernel,
        out_shape=(
            jax.ShapeDtypeStruct((MINE, LAT_KV), bf16),
            jax.ShapeDtypeStruct((8, 128), f32),
        ),
        in_specs=[VMEM] * 2,
        out_specs=(VMEM, VMEM),
        compiler_params=params(),
        name="own_attention",
    )(query, keys)


def combine_kernel(arrived, own_latents, own_stats, value_up, out):
    bests, totals = [own_stats[0:1, :]], [own_stats[1:2, :]]
    for z in range(NEAR):
        stats = arrived[z, MINE:, :128].astype(f32)
        bests.append(stats[0:1] + stats[1:2] + stats[2:3])
        totals.append(stats[3:4] + stats[4:5] + stats[5:6])
    top = bests[0]
    for best in bests[1:]:
        top = jnp.maximum(top, best)
    shares = [total * jnp.exp(best - top) for best, total in zip(bests, totals)]
    whole = shares[0]
    for share in shares[1:]:
        whole = whole + share
    index = lax.broadcasted_iota(jnp.int32, (128, 128), 0)
    table = jnp.zeros((128, 128), f32)
    for i, share in enumerate(shares):
        table = jnp.where(index == i, jnp.broadcast_to(share / whole, (128, 128)), table)
    table = jnp.transpose(table)
    latent = table[:, 0:1] * own_latents[...].astype(f32)
    for z in range(NEAR):
        latent = latent + table[:, z + 1 : z + 2] * arrived[z, :MINE, :].astype(f32)
    latent = latent.astype(bf16)
    for head in range(2):
        values = dot(latent[head * ROWS : (head + 1) * ROWS], value_up[head])
        out[:, head * HEAD_V : (head + 1) * HEAD_V] = values.astype(bf16)


def combine(arrived, own_latents, own_stats, value_up):
    return pl.pallas_call(
        combine_kernel,
        out_shape=jax.ShapeDtypeStruct((ROWS, 2 * HEAD_V), bf16),
        in_specs=[VMEM] * 4,
        out_specs=VMEM,
        compiler_params=params(),
        name="combine",
    )(arrived, own_latents, own_stats, value_up)


def project_kernel(head_values, weight, out):
    for i in range(NEAR):
        out[i] = dot(head_values[...], weight[:, i * SPAN : (i + 1) * SPAN]).astype(bf16)


def project(head_values, weight):
    return pl.pallas_call(
        project_kernel,
        out_shape=jax.ShapeDtypeStruct((NEAR, ROWS, SPAN), bf16),
        in_specs=[VMEM] * 2,
        out_specs=VMEM,
        compiler_params=params(),
        name="project",
    )(head_values, weight)


def add_kernel(arrived, out):
    total = arrived[0].astype(f32)
    for i in range(1, NEAR):
        total = total + arrived[i].astype(f32)
    total = total.astype(bf16)
    for q in range(NQ):
        out[q] = total


def add(arrived):
    return pl.pallas_call(
        add_kernel,
        out_shape=jax.ShapeDtypeStruct((NQ, ROWS, SPAN), bf16),
        in_specs=[VMEM],
        out_specs=VMEM,
        compiler_params=params(),
        name="add",
    )(arrived)


def slots_kernel(routes, gates, picks, slot_gates):
    slot = lax.broadcasted_iota(jnp.int32, (SLOTS, ROWS), 0)
    expert = lax.shift_right_logical(slot, 1)
    chosen = jnp.zeros((SLOTS, ROWS), f32)
    gating = jnp.zeros((SLOTS, ROWS), f32)
    for k in range(8):
        match = expert == routes[k : k + 1, :]
        chosen = jnp.where(match, 1.0, chosen)
        gating = jnp.where(match, gates[k : k + 1, :], gating)
    earlier = lax.broadcasted_iota(jnp.int32, (ROWS, ROWS), 0) < lax.broadcasted_iota(
        jnp.int32, (ROWS, ROWS), 1
    )
    position = dot(chosen.astype(bf16), jnp.where(earlier, 1.0, 0.0).astype(bf16))
    place = (slot & 1).astype(f32)
    selected = jnp.where(position == place, chosen, 0.0)
    picks[...] = selected.astype(bf16)
    slot_gates[...] = jnp.sum(selected * gating, axis=1, keepdims=True)


def slots(routes, gates):
    return pl.pallas_call(
        slots_kernel,
        out_shape=(
            jax.ShapeDtypeStruct((SLOTS, ROWS), bf16),
            jax.ShapeDtypeStruct((SLOTS, 1), f32),
        ),
        in_specs=[VMEM] * 2,
        out_specs=(VMEM, VMEM),
        compiler_params=params(),
        name="slots",
    )(routes, gates)


def dispatch_kernel(zq, arrived, picks, out):
    total = arrived[0].astype(f32)
    for q in range(1, NQ):
        total = total + arrived[q].astype(f32)
    first = pl.multiple_of(zq[0] * NEAR_SLOTS, NEAR_SLOTS)
    out[...] = dot(picks[pl.ds(first, NEAR_SLOTS), :], total.astype(bf16)).astype(bf16)


def dispatch(zq, arrived, picks):
    return pl.pallas_call(
        dispatch_kernel,
        out_shape=jax.ShapeDtypeStruct((NEAR_SLOTS, SPAN), bf16),
        in_specs=[SMEM, VMEM, VMEM],
        out_specs=VMEM,
        compiler_params=params(),
        name="dispatch",
    )(zq, arrived, picks)


def norm_kernel(arrived, gain, out):
    square = jnp.zeros((OWN_SLOTS, 128), f32)
    for i in range(NEAR):
        block = arrived[i].astype(f32)
        for lane in range(0, SPAN, 128):
            part = block[:, lane : lane + 128]
            square = square + part * part
    scale = lax.rsqrt(jnp.sum(square, axis=1, keepdims=True) * (1.0 / D) + EPSILON)
    for i in range(NEAR):
        part = slice(i * SPAN, (i + 1) * SPAN)
        normed = arrived[i].astype(f32) * scale * gain[:, part].astype(f32)
        for expert in range(OWN_SLOTS // CAP):
            out[expert, :, part] = normed[expert * CAP : (expert + 1) * CAP]


def norm(arrived, gain):
    return pl.pallas_call(
        norm_kernel,
        out_shape=jax.ShapeDtypeStruct((OWN_SLOTS // CAP, CAP, D), f32),
        in_specs=[VMEM] * 2,
        out_specs=VMEM,
        compiler_params=params(),
        name="norm",
    )(arrived, gain)


def exchange(value, axes):
    return lax.all_to_all(value, axes, split_axis=0, concat_axis=0, tiled=True)


def local(
    prompt_cache,
    prompt_of_group,
    queries,
    new_latents,
    value_up,
    out_weight,
    norm_gain,
    routes,
    gates,
):
    core = lax.axis_index("core")[None].astype(jnp.int32)
    zq = lax.axis_index("zq")[None].astype(jnp.int32)
    zl = lax.axis_index("zl")[None].astype(jnp.int32)
    dev = (lax.axis_index("zq") * NL + lax.axis_index("zl")) * NX + lax.axis_index("x")
    swap = [(0, 1), (1, 0)]

    query = queries.reshape(ROWS, 2, LAT).transpose(1, 0, 2).reshape(MINE, LAT)
    pieces = exchange(prompt_cache.reshape(NY, PIECE, LAT), "y")
    pieces, query = lax.optimization_barrier((pieces, query))
    all_queries = exchange(jnp.broadcast_to(query, (NX, MINE, LAT)), "x")
    other = lax.ppermute(pieces, "core", swap)
    wanted = jnp.where(core[0] == 0, prompt_of_group[0::2], prompt_of_group[1::2])
    picked = pick(core, wanted, pieces, other)
    picked, all_queries = lax.optimization_barrier((picked, all_queries))
    other_queries = lax.ppermute(all_queries, "zl", swap)
    served = exchange(picked, "y").reshape(NY * PIECE, LAT)
    keys = lax.all_gather(served, "zq", axis=0, tiled=True)
    own_latents, own_stats = own_attention(query, new_latents.reshape(ROWS, LAT))
    picks, all_gates = slots(routes.T, gates.T)
    slot_gates = lax.dynamic_slice_in_dim(all_gates, dev * OWN_SLOTS, OWN_SLOTS, 0)

    partial = exchange(prompt_attention(zl, all_queries, other_queries, keys), ("zl", "x"))
    head_values = combine(partial, own_latents, own_stats, value_up)
    sums = exchange(add(exchange(project(head_values, out_weight), ("zl", "x"))), "zq")
    rows = dispatch(zq, sums, picks).reshape(NEAR, OWN_SLOTS, SPAN)
    slot_rows = norm(exchange(rows, ("zl", "x")), norm_gain.reshape(1, D))
    return (slot_rows[None], slot_gates.reshape(1, OWN_SLOTS // CAP, CAP))


def solution(mesh):
    axes = ("y", "core", "zq", "zl", "x")
    fine = Mesh(mesh.devices.reshape(NY, 2, NQ, NL, NX), axes)
    group, dev = axes[:2], axes[2:]
    return jax.shard_map(
        local,
        mesh=fine,
        in_specs=(
            P(group, dev, None),
            P(),
            P(group, None, None, dev, None),
            P(group, None, None, None),
            P(dev, None, None),
            P(dev, None),
            P(),
            P(group, None),
            P(group, None),
        ),
        out_specs=(P(group, dev, None, None), P(group, dev, None)),
        check_vma=False,
    )
```

```python
import jax
import jax.numpy as jnp
from jax import lax
from jax.experimental import pallas as pl
from jax.experimental.pallas import tpu as pltpu
from jax.sharding import Mesh
from jax.sharding import PartitionSpec as P

D = 7168
LAT = 576
LAT_KV = 512
HEAD_V = 128
QK_DIM = 192
EXPERTS = 384
CAP = 2
ROWS = 64
EPSILON = 1e-06
SCALE = QK_DIM ** (-0.5)

NY, NQ, NL, NX = 8, 4, 2, 4
NEAR = NL * NX
DEVS = NQ * NEAR
PIECE = 192 // NY
KEYS = 192 * NQ
MINE = 2 * ROWS
SENT = MINE + 16
SLOTS = EXPERTS * CAP
OWN_SLOTS = SLOTS // DEVS
NEAR_SLOTS = NEAR * OWN_SLOTS
SPAN = D // NEAR
FOUR = 4
PACKED = LAT_KV // 128 * MINE + ROWS

bf16 = jnp.bfloat16
f32 = jnp.float32
VMEM = pl.BlockSpec(memory_space=pltpu.VMEM)
SMEM = pl.BlockSpec(memory_space=pltpu.SMEM)


def params(mib=24):
    return pltpu.CompilerParams(vmem_limit_bytes=mib * 1024 * 1024)


def cost(micros):
    return pl.CostEstimate(flops=0, bytes_accessed=3_000_000 * micros, transcendentals=0)


def dot(a, b, dims=((1,), (0,))):
    return lax.dot_general(a, b, (dims, ((), ())), preferred_element_type=f32)


def columns_to_lanes(column):
    return jnp.transpose(jnp.broadcast_to(column, (MINE, 128)))[:1]


def pick_kernel(core, wanted, mine, other, out):
    for y in range(NY):
        prompt = wanted[y]
        row = lax.shift_right_logical(prompt, 1)

        @pl.when((prompt & 1) == core[0])
        def _():
            out[y] = mine[row]

        @pl.when((prompt & 1) != core[0])
        def _():
            out[y] = other[row]


def pick(core, wanted, mine, other):
    return pl.pallas_call(
        pick_kernel,
        out_shape=jax.ShapeDtypeStruct(mine.shape, mine.dtype),
        in_specs=[SMEM, SMEM, VMEM, VMEM],
        out_specs=VMEM,
        compiler_params=params(),
        name="pick",
    )(core, wanted, mine, other)


def spread_kernel(query, copies, single):
    heads = [query[:, head, :] for head in range(2)]
    rest = jnp.concatenate([head[:, LAT_KV:] for head in heads], axis=1)
    for head in range(2):
        single[head * ROWS : (head + 1) * ROWS, :] = heads[head]
    for i in range(FOUR):
        for tile in range(LAT_KV // 128):
            for head in range(2):
                first = tile * MINE + head * ROWS
                copies[i, first : first + ROWS, :] = heads[head][:, tile * 128 : (tile + 1) * 128]
        copies[i, PACKED - ROWS :, :] = rest


def spread(query):
    return pl.pallas_call(
        spread_kernel,
        out_shape=(
            jax.ShapeDtypeStruct((FOUR, PACKED, 128), bf16),
            jax.ShapeDtypeStruct((MINE, LAT), bf16),
        ),
        in_specs=[VMEM],
        out_specs=(VMEM, VMEM),
        compiler_params=params(),
        cost_estimate=cost(2),
        name="spread",
    )(query)


def unpacked(packed, i):
    tiles = [packed[i, tile * MINE : (tile + 1) * MINE, :] for tile in range(LAT_KV // 128)]
    rest = packed[i, PACKED - ROWS :, :]
    width = LAT - LAT_KV
    tiles.append(jnp.concatenate([rest[:, :width], rest[:, width:]], axis=0))
    return jnp.concatenate(tiles, axis=1)


def attend(query, keys, visible=None):
    scores = dot(query, keys, ((1,), (1,))) * SCALE
    if visible is not None:
        scores = jnp.where(visible, scores, -1e30)
    best = jnp.max(scores, axis=1, keepdims=True)
    weights = jnp.exp(scores - best)
    total = jnp.sum(weights, axis=1, keepdims=True)
    latent = dot(weights.astype(bf16), keys[:, :LAT_KV]) / total
    return best, total, latent.astype(bf16)


def three(value):
    high = value.astype(bf16).astype(f32)
    rest = value - high
    mid = rest.astype(bf16).astype(f32)
    return high, mid, rest - mid


def attention_kernel(xh, mine, other, keys, out):
    index = lax.broadcasted_iota(jnp.int32, (16, 128), 0)
    for step in range(NL):
        queries = (mine, other)[step]
        first = (xh[0] ^ step) * 2
        query = jnp.concatenate([unpacked(queries, i) for i in range(FOUR)], axis=0)
        best, total, latent = attend(query, keys[...])
        for i in range(FOUR):
            part = slice(i * MINE, (i + 1) * MINE)
            owner = first + (i // 2) * NX + i % 2
            out[owner, :MINE, :] = latent[part]
            rows = three(columns_to_lanes(best[part])) + three(columns_to_lanes(total[part]))
            table = jnp.zeros((16, 128), f32)
            for j, row in enumerate(rows):
                table = jnp.where(index == j, jnp.broadcast_to(row, (16, 128)), table)
            out[owner, MINE:, :128] = table.astype(bf16)
            out[owner, MINE:, 128:] = jnp.zeros((16, LAT_KV - 128), bf16)


def prompt_attention(xh, mine, other, keys):
    return pl.pallas_call(
        attention_kernel,
        out_shape=jax.ShapeDtypeStruct((NEAR, SENT, LAT_KV), bf16),
        in_specs=[SMEM] + [VMEM] * 3,
        out_specs=VMEM,
        compiler_params=params(),
        name="prompt_attention",
    )(xh, mine, other, keys)


def own_kernel(query, keys, latents, stats):
    row = lax.broadcasted_iota(jnp.int32, (MINE, ROWS), 0) & (ROWS - 1)
    key = lax.broadcasted_iota(jnp.int32, (MINE, ROWS), 1)
    same = lax.shift_right_logical(row, 2) == lax.shift_right_logical(key, 2)
    best, total, latent = attend(query[...], keys[...], same & (key <= row))
    latents[...] = latent
    index = lax.broadcasted_iota(jnp.int32, (8, 128), 0)
    stats[...] = jnp.where(
        index == 0,
        jnp.broadcast_to(columns_to_lanes(best), (8, 128)),
        jnp.broadcast_to(columns_to_lanes(total), (8, 128)),
    )


def own_attention(query, keys):
    return pl.pallas_call(
        own_kernel,
        out_shape=(
            jax.ShapeDtypeStruct((MINE, LAT_KV), bf16),
            jax.ShapeDtypeStruct((8, 128), f32),
        ),
        in_specs=[VMEM] * 2,
        out_specs=(VMEM, VMEM),
        compiler_params=params(),
        name="own_attention",
    )(query, keys)


def combine_kernel(arrived, own_latents, own_stats, value_up, out):
    bests, totals = [own_stats[0:1, :]], [own_stats[1:2, :]]
    for z in range(NEAR):
        stats = arrived[z, MINE:, :128].astype(f32)
        bests.append(stats[0:1] + stats[1:2] + stats[2:3])
        totals.append(stats[3:4] + stats[4:5] + stats[5:6])
    top = bests[0]
    for best in bests[1:]:
        top = jnp.maximum(top, best)
    shares = [total * jnp.exp(best - top) for best, total in zip(bests, totals)]
    whole = shares[0]
    for share in shares[1:]:
        whole = whole + share
    index = lax.broadcasted_iota(jnp.int32, (128, 128), 0)
    table = jnp.zeros((128, 128), f32)
    for i, share in enumerate(shares):
        table = jnp.where(index == i, jnp.broadcast_to(share / whole, (128, 128)), table)
    table = jnp.transpose(table)
    latent = table[:, 0:1] * own_latents[...].astype(f32)
    for z in range(NEAR):
        latent = latent + table[:, z + 1 : z + 2] * arrived[z, :MINE, :].astype(f32)
    latent = latent.astype(bf16)
    for head in range(2):
        values = dot(latent[head * ROWS : (head + 1) * ROWS], value_up[head])
        out[:, head * HEAD_V : (head + 1) * HEAD_V] = values.astype(bf16)


def combine(arrived, own_latents, own_stats, value_up):
    return pl.pallas_call(
        combine_kernel,
        out_shape=jax.ShapeDtypeStruct((ROWS, 2 * HEAD_V), bf16),
        in_specs=[VMEM] * 4,
        out_specs=VMEM,
        compiler_params=params(),
        name="combine",
    )(arrived, own_latents, own_stats, value_up)


def project_kernel(head_values, weight, out):
    for i in range(NEAR):
        out[i] = dot(head_values[...], weight[:, i * SPAN : (i + 1) * SPAN]).astype(bf16)


def project(head_values, weight):
    return pl.pallas_call(
        project_kernel,
        out_shape=jax.ShapeDtypeStruct((NEAR, ROWS, SPAN), bf16),
        in_specs=[VMEM] * 2,
        out_specs=VMEM,
        compiler_params=params(),
        name="project",
    )(head_values, weight)


def add_kernel(arrived, out):
    total = arrived[0].astype(f32)
    for i in range(1, NEAR):
        total = total + arrived[i].astype(f32)
    total = total.astype(bf16)
    for q in range(NQ):
        out[q] = total


def add(arrived):
    return pl.pallas_call(
        add_kernel,
        out_shape=jax.ShapeDtypeStruct((NQ, ROWS, SPAN), bf16),
        in_specs=[VMEM],
        out_specs=VMEM,
        compiler_params=params(),
        name="add",
    )(arrived)


def slots_kernel(routes, gates, picks, slot_gates):
    slot = lax.broadcasted_iota(jnp.int32, (SLOTS, ROWS), 0)
    expert = lax.shift_right_logical(slot, 1)
    chosen = jnp.zeros((SLOTS, ROWS), f32)
    gating = jnp.zeros((SLOTS, ROWS), f32)
    for k in range(8):
        match = expert == routes[k : k + 1, :]
        chosen = jnp.where(match, 1.0, chosen)
        gating = jnp.where(match, gates[k : k + 1, :], gating)
    earlier = lax.broadcasted_iota(jnp.int32, (ROWS, ROWS), 0) < lax.broadcasted_iota(
        jnp.int32, (ROWS, ROWS), 1
    )
    position = dot(chosen.astype(bf16), jnp.where(earlier, 1.0, 0.0).astype(bf16))
    place = (slot & 1).astype(f32)
    selected = jnp.where(position == place, chosen, 0.0)
    picks[...] = selected.astype(bf16)
    slot_gates[...] = jnp.sum(selected * gating, axis=1, keepdims=True)


def slots(routes, gates):
    return pl.pallas_call(
        slots_kernel,
        out_shape=(
            jax.ShapeDtypeStruct((SLOTS, ROWS), bf16),
            jax.ShapeDtypeStruct((SLOTS, 1), f32),
        ),
        in_specs=[VMEM] * 2,
        out_specs=(VMEM, VMEM),
        compiler_params=params(),
        name="slots",
    )(routes, gates)


def dispatch_kernel(zq, arrived, picks, out):
    total = arrived[0].astype(f32)
    for q in range(1, NQ):
        total = total + arrived[q].astype(f32)
    first = pl.multiple_of(zq[0] * NEAR_SLOTS, NEAR_SLOTS)
    out[...] = dot(picks[pl.ds(first, NEAR_SLOTS), :], total.astype(bf16)).astype(bf16)


def dispatch(zq, arrived, picks):
    return pl.pallas_call(
        dispatch_kernel,
        out_shape=jax.ShapeDtypeStruct((NEAR_SLOTS, SPAN), bf16),
        in_specs=[SMEM, VMEM, VMEM],
        out_specs=VMEM,
        compiler_params=params(),
        name="dispatch",
    )(zq, arrived, picks)


def norm_kernel(arrived, gain, out):
    square = jnp.zeros((OWN_SLOTS, 128), f32)
    for i in range(NEAR):
        block = arrived[i].astype(f32)
        for lane in range(0, SPAN, 128):
            part = block[:, lane : lane + 128]
            square = square + part * part
    scale = lax.rsqrt(jnp.sum(square, axis=1, keepdims=True) * (1.0 / D) + EPSILON)
    for i in range(NEAR):
        part = slice(i * SPAN, (i + 1) * SPAN)
        normed = arrived[i].astype(f32) * scale * gain[:, part].astype(f32)
        for expert in range(OWN_SLOTS // CAP):
            out[expert, :, part] = normed[expert * CAP : (expert + 1) * CAP]


def norm(arrived, gain):
    return pl.pallas_call(
        norm_kernel,
        out_shape=jax.ShapeDtypeStruct((OWN_SLOTS // CAP, CAP, D), f32),
        in_specs=[VMEM] * 2,
        out_specs=VMEM,
        compiler_params=params(),
        name="norm",
    )(arrived, gain)


def exchange(value, axes):
    return lax.all_to_all(value, axes, split_axis=0, concat_axis=0, tiled=True)


def local(
    prompt_cache,
    prompt_of_group,
    queries,
    new_latents,
    value_up,
    out_weight,
    norm_gain,
    routes,
    gates,
):
    core = lax.axis_index("core")[None].astype(jnp.int32)
    zq = lax.axis_index("zq")[None].astype(jnp.int32)
    xh = lax.axis_index("xh")[None].astype(jnp.int32)
    dev = (lax.axis_index("zq") * NL + lax.axis_index("zl")) * NX + (lax.axis_index("xh") * 2 + lax.axis_index("xl"))
    swap = [(0, 1), (1, 0)]

    copies, query = spread(queries.reshape(ROWS, 2, LAT))
    pieces = exchange(prompt_cache.reshape(NY, PIECE, LAT), "y")
    pieces, copies = lax.optimization_barrier((pieces, copies))
    all_queries = exchange(copies, ("zl", "xl"))
    other = lax.ppermute(pieces, "core", swap)
    wanted = jnp.where(core[0] == 0, prompt_of_group[0::2], prompt_of_group[1::2])
    picked = pick(core, wanted, pieces, other)
    picked, all_queries = lax.optimization_barrier((picked, all_queries))
    other_queries = lax.ppermute(all_queries, "xh", swap)
    served = exchange(picked, "y").reshape(NY * PIECE, LAT)
    keys = lax.all_gather(served, "zq", axis=0, tiled=True)
    own_latents, own_stats = own_attention(query, new_latents.reshape(ROWS, LAT))
    picks, all_gates = slots(routes.T, gates.T)
    slot_gates = lax.dynamic_slice_in_dim(all_gates, dev * OWN_SLOTS, OWN_SLOTS, 0)

    partial = exchange(prompt_attention(xh, all_queries, other_queries, keys), ("zl", "xh", "xl"))
    head_values = combine(partial, own_latents, own_stats, value_up)
    sums = exchange(add(exchange(project(head_values, out_weight), ("zl", "xh", "xl"))), "zq")
    rows = dispatch(zq, sums, picks).reshape(NEAR, OWN_SLOTS, SPAN)
    slot_rows = norm(exchange(rows, ("zl", "xh", "xl")), norm_gain.reshape(1, D))
    return (slot_rows[None], slot_gates.reshape(1, OWN_SLOTS // CAP, CAP))


def solution(mesh):
    axes = ("y", "core", "zq", "zl", "xh", "xl")
    fine = Mesh(mesh.devices.reshape(NY, 2, NQ, NL, 2, NX // 2), axes)
    group, dev = axes[:2], axes[2:]
    return jax.shard_map(
        local,
        mesh=fine,
        in_specs=(
            P(group, dev, None),
            P(),
            P(group, None, None, dev, None),
            P(group, None, None, None),
            P(dev, None, None),
            P(dev, None),
            P(),
            P(group, None),
            P(group, None),
        ),
        out_specs=(P(group, dev, None, None), P(group, dev, None)),
        check_vma=False,
    )
```

```python
import jax
import jax.numpy as jnp
from jax import lax
from jax.experimental import pallas as pl
from jax.experimental.pallas import tpu as pltpu
from jax.sharding import Mesh
from jax.sharding import PartitionSpec as P

D = 7168
LAT = 576
LAT_KV = 512
HEAD_V = 128
QK_DIM = 192
EXPERTS = 384
CAP = 2
ROWS = 64
EPSILON = 1e-06
SCALE = QK_DIM ** (-0.5)

NY, NQ, NL, NX = 8, 4, 2, 4
NEAR = NL * NX
DEVS = NQ * NEAR
PIECE = 192 // NY
KEYS = 192 * NQ
MINE = 2 * ROWS
LANES = LAT_KV // 128
STATS = LANES * MINE
SENT = STATS + 16
SLOTS = EXPERTS * CAP
OWN_SLOTS = SLOTS // DEVS
NEAR_SLOTS = NEAR * OWN_SLOTS
SPAN = D // NEAR
FOUR = 4
PACKED = LAT_KV // 128 * MINE + ROWS

bf16 = jnp.bfloat16
f32 = jnp.float32
VMEM = pl.BlockSpec(memory_space=pltpu.VMEM)
SMEM = pl.BlockSpec(memory_space=pltpu.SMEM)


def params(mib=24):
    return pltpu.CompilerParams(vmem_limit_bytes=mib * 1024 * 1024)


def cost(micros):
    return pl.CostEstimate(flops=0, bytes_accessed=3_000_000 * micros, transcendentals=0)


def dot(a, b, dims=((1,), (0,))):
    return lax.dot_general(a, b, (dims, ((), ())), preferred_element_type=f32)


def columns_to_lanes(column):
    return jnp.transpose(jnp.broadcast_to(column, (MINE, 128)))[:1]


def pick_kernel(core, wanted, mine, other, out):
    for y in range(NY):
        prompt = wanted[y]
        row = lax.shift_right_logical(prompt, 1)

        @pl.when((prompt & 1) == core[0])
        def _():
            out[y] = mine[row]

        @pl.when((prompt & 1) != core[0])
        def _():
            out[y] = other[row]


def pick(core, wanted, mine, other):
    return pl.pallas_call(
        pick_kernel,
        out_shape=jax.ShapeDtypeStruct(mine.shape, mine.dtype),
        in_specs=[SMEM, SMEM, VMEM, VMEM],
        out_specs=VMEM,
        compiler_params=params(),
        name="pick",
    )(core, wanted, mine, other)


def spread_kernel(query, copies, single):
    heads = [query[:, head, :] for head in range(2)]
    rest = jnp.concatenate([head[:, LAT_KV:] for head in heads], axis=1)
    for head in range(2):
        single[head * ROWS : (head + 1) * ROWS, :] = heads[head]
    for i in range(FOUR):
        for tile in range(LAT_KV // 128):
            for head in range(2):
                first = tile * MINE + head * ROWS
                copies[i, first : first + ROWS, :] = heads[head][:, tile * 128 : (tile + 1) * 128]
        copies[i, PACKED - ROWS :, :] = rest


def spread(query):
    return pl.pallas_call(
        spread_kernel,
        out_shape=(
            jax.ShapeDtypeStruct((FOUR, PACKED, 128), bf16),
            jax.ShapeDtypeStruct((MINE, LAT), bf16),
        ),
        in_specs=[VMEM],
        out_specs=(VMEM, VMEM),
        compiler_params=params(),
        cost_estimate=cost(2),
        name="spread",
    )(query)


def unpacked(packed, i):
    tiles = [packed[i, tile * MINE : (tile + 1) * MINE, :] for tile in range(LAT_KV // 128)]
    rest = packed[i, PACKED - ROWS :, :]
    width = LAT - LAT_KV
    tiles.append(jnp.concatenate([rest[:, :width], rest[:, width:]], axis=0))
    return jnp.concatenate(tiles, axis=1)


def attend(query, keys, visible=None):
    scores = dot(query, keys, ((1,), (1,))) * SCALE
    if visible is not None:
        scores = jnp.where(visible, scores, -1e30)
    best = jnp.max(scores, axis=1, keepdims=True)
    weights = jnp.exp(scores - best)
    total = jnp.sum(weights, axis=1, keepdims=True)
    latent = dot(weights.astype(bf16), keys[:, :LAT_KV]) / total
    return best, total, latent.astype(bf16)


def three(value):
    high = value.astype(bf16).astype(f32)
    rest = value - high
    mid = rest.astype(bf16).astype(f32)
    return high, mid, rest - mid


def attention_kernel(xh, mine, other, keys, out):
    index = lax.broadcasted_iota(jnp.int32, (16, 128), 0)
    for step in range(1):
        query = jnp.concatenate(
            [unpacked(queries, i) for queries in (mine, other) for i in range(FOUR)], axis=0
        )
        best, total, latent = attend(query, keys[...])
        for i in range(2 * FOUR):
            part = slice(i * MINE, (i + 1) * MINE)
            owner = (xh[0] ^ (i // FOUR)) * 2 + (i % FOUR // 2) * NX + i % 2
            for tile in range(LANES):
                lanes = slice(tile * 128, (tile + 1) * 128)
                out[owner, tile * MINE : (tile + 1) * MINE, :] = latent[part, lanes]
            rows = three(columns_to_lanes(best[part])) + three(columns_to_lanes(total[part]))
            table = jnp.zeros((16, 128), f32)
            for j, row in enumerate(rows):
                table = jnp.where(index == j, jnp.broadcast_to(row, (16, 128)), table)
            out[owner, STATS:, :] = table.astype(bf16)


def prompt_attention(xh, mine, other, keys):
    return pl.pallas_call(
        attention_kernel,
        out_shape=jax.ShapeDtypeStruct((NEAR, SENT, 128), bf16),
        in_specs=[SMEM] + [VMEM] * 3,
        out_specs=VMEM,
        compiler_params=params(),
        name="prompt_attention",
    )(xh, mine, other, keys)


def own_kernel(query, keys, latents, stats):
    row = lax.broadcasted_iota(jnp.int32, (MINE, ROWS), 0) & (ROWS - 1)
    key = lax.broadcasted_iota(jnp.int32, (MINE, ROWS), 1)
    same = lax.shift_right_logical(row, 2) == lax.shift_right_logical(key, 2)
    best, total, latent = attend(query[...], keys[...], same & (key <= row))
    latents[...] = latent
    index = lax.broadcasted_iota(jnp.int32, (8, 128), 0)
    stats[...] = jnp.where(
        index == 0,
        jnp.broadcast_to(columns_to_lanes(best), (8, 128)),
        jnp.broadcast_to(columns_to_lanes(total), (8, 128)),
    )


def own_attention(query, keys):
    return pl.pallas_call(
        own_kernel,
        out_shape=(
            jax.ShapeDtypeStruct((MINE, LAT_KV), bf16),
            jax.ShapeDtypeStruct((8, 128), f32),
        ),
        in_specs=[VMEM] * 2,
        out_specs=(VMEM, VMEM),
        compiler_params=params(),
        name="own_attention",
    )(query, keys)


def combine_kernel(arrived, own_latents, own_stats, value_up, out):
    bests, totals = [own_stats[0:1, :]], [own_stats[1:2, :]]
    for z in range(NEAR):
        stats = arrived[z, STATS:, :].astype(f32)
        bests.append(stats[0:1] + stats[1:2] + stats[2:3])
        totals.append(stats[3:4] + stats[4:5] + stats[5:6])
    top = bests[0]
    for best in bests[1:]:
        top = jnp.maximum(top, best)
    shares = [total * jnp.exp(best - top) for best, total in zip(bests, totals)]
    whole = shares[0]
    for share in shares[1:]:
        whole = whole + share
    index = lax.broadcasted_iota(jnp.int32, (128, 128), 0)
    table = jnp.zeros((128, 128), f32)
    for i, share in enumerate(shares):
        table = jnp.where(index == i, jnp.broadcast_to(share / whole, (128, 128)), table)
    table = jnp.transpose(table)
    tiles = []
    for tile in range(LANES):
        lanes = slice(tile * 128, (tile + 1) * 128)
        latent = table[:, 0:1] * own_latents[:, lanes].astype(f32)
        for z in range(NEAR):
            part = arrived[z, tile * MINE : (tile + 1) * MINE, :].astype(f32)
            latent = latent + table[:, z + 1 : z + 2] * part
        tiles.append(latent.astype(bf16))
    latent = jnp.concatenate(tiles, axis=1)
    for head in range(2):
        values = dot(latent[head * ROWS : (head + 1) * ROWS], value_up[head])
        out[:, head * HEAD_V : (head + 1) * HEAD_V] = values.astype(bf16)


def combine(arrived, own_latents, own_stats, value_up):
    return pl.pallas_call(
        combine_kernel,
        out_shape=jax.ShapeDtypeStruct((ROWS, 2 * HEAD_V), bf16),
        in_specs=[VMEM] * 4,
        out_specs=VMEM,
        compiler_params=params(),
        name="combine",
    )(arrived, own_latents, own_stats, value_up)


def project_kernel(head_values, weight, out):
    for i in range(NEAR):
        out[i] = dot(head_values[...], weight[:, i * SPAN : (i + 1) * SPAN]).astype(bf16)


def project(head_values, weight):
    return pl.pallas_call(
        project_kernel,
        out_shape=jax.ShapeDtypeStruct((NEAR, ROWS, SPAN), bf16),
        in_specs=[VMEM] * 2,
        out_specs=VMEM,
        compiler_params=params(),
        name="project",
    )(head_values, weight)


def add_kernel(arrived, out):
    total = arrived[0].astype(f32)
    for i in range(1, NEAR):
        total = total + arrived[i].astype(f32)
    total = total.astype(bf16)
    for q in range(NQ):
        out[q] = total


def add(arrived):
    return pl.pallas_call(
        add_kernel,
        out_shape=jax.ShapeDtypeStruct((NQ, ROWS, SPAN), bf16),
        in_specs=[VMEM],
        out_specs=VMEM,
        compiler_params=params(),
        name="add",
    )(arrived)


def slots_kernel(routes, gates, picks, slot_gates):
    slot = lax.broadcasted_iota(jnp.int32, (SLOTS, ROWS), 0)
    expert = lax.shift_right_logical(slot, 1)
    chosen = jnp.zeros((SLOTS, ROWS), f32)
    gating = jnp.zeros((SLOTS, ROWS), f32)
    for k in range(8):
        match = expert == routes[k : k + 1, :]
        chosen = jnp.where(match, 1.0, chosen)
        gating = jnp.where(match, gates[k : k + 1, :], gating)
    earlier = lax.broadcasted_iota(jnp.int32, (ROWS, ROWS), 0) < lax.broadcasted_iota(
        jnp.int32, (ROWS, ROWS), 1
    )
    position = dot(chosen.astype(bf16), jnp.where(earlier, 1.0, 0.0).astype(bf16))
    place = (slot & 1).astype(f32)
    selected = jnp.where(position == place, chosen, 0.0)
    picks[...] = selected.astype(bf16)
    slot_gates[...] = jnp.sum(selected * gating, axis=1, keepdims=True)


def slots(routes, gates):
    return pl.pallas_call(
        slots_kernel,
        out_shape=(
            jax.ShapeDtypeStruct((SLOTS, ROWS), bf16),
            jax.ShapeDtypeStruct((SLOTS, 1), f32),
        ),
        in_specs=[VMEM] * 2,
        out_specs=(VMEM, VMEM),
        compiler_params=params(),
        name="slots",
    )(routes, gates)


def dispatch_kernel(zq, arrived, picks, out):
    total = arrived[0].astype(f32)
    for q in range(1, NQ):
        total = total + arrived[q].astype(f32)
    first = pl.multiple_of(zq[0] * NEAR_SLOTS, NEAR_SLOTS)
    out[...] = dot(picks[pl.ds(first, NEAR_SLOTS), :], total.astype(bf16)).astype(bf16)


def dispatch(zq, arrived, picks):
    return pl.pallas_call(
        dispatch_kernel,
        out_shape=jax.ShapeDtypeStruct((NEAR_SLOTS, SPAN), bf16),
        in_specs=[SMEM, VMEM, VMEM],
        out_specs=VMEM,
        compiler_params=params(),
        name="dispatch",
    )(zq, arrived, picks)


def norm_kernel(arrived, gain, out):
    square = jnp.zeros((OWN_SLOTS, 128), f32)
    for i in range(NEAR):
        block = arrived[i].astype(f32)
        for lane in range(0, SPAN, 128):
            part = block[:, lane : lane + 128]
            square = square + part * part
    scale = lax.rsqrt(jnp.sum(square, axis=1, keepdims=True) * (1.0 / D) + EPSILON)
    for i in range(NEAR):
        part = slice(i * SPAN, (i + 1) * SPAN)
        normed = arrived[i].astype(f32) * scale * gain[:, part].astype(f32)
        for expert in range(OWN_SLOTS // CAP):
            out[expert, :, part] = normed[expert * CAP : (expert + 1) * CAP]


def norm(arrived, gain):
    return pl.pallas_call(
        norm_kernel,
        out_shape=jax.ShapeDtypeStruct((OWN_SLOTS // CAP, CAP, D), f32),
        in_specs=[VMEM] * 2,
        out_specs=VMEM,
        compiler_params=params(),
        name="norm",
    )(arrived, gain)


def exchange(value, axes):
    return lax.all_to_all(value, axes, split_axis=0, concat_axis=0, tiled=True)


def local(
    prompt_cache,
    prompt_of_group,
    queries,
    new_latents,
    value_up,
    out_weight,
    norm_gain,
    routes,
    gates,
):
    core = lax.axis_index("core")[None].astype(jnp.int32)
    zq = lax.axis_index("zq")[None].astype(jnp.int32)
    xh = lax.axis_index("xh")[None].astype(jnp.int32)
    dev = (lax.axis_index("zq") * NL + lax.axis_index("zl")) * NX + (lax.axis_index("xh") * 2 + lax.axis_index("xl"))
    swap = [(0, 1), (1, 0)]

    copies, query = spread(queries.reshape(ROWS, 2, LAT))
    pieces = exchange(prompt_cache.reshape(NY, PIECE, LAT), "y")
    pieces, copies = lax.optimization_barrier((pieces, copies))
    all_queries = exchange(copies, ("zl", "xl"))
    other = lax.ppermute(pieces, "core", swap)
    wanted = jnp.where(core[0] == 0, prompt_of_group[0::2], prompt_of_group[1::2])
    picked = pick(core, wanted, pieces, other)
    picked, all_queries = lax.optimization_barrier((picked, all_queries))
    other_queries = lax.ppermute(all_queries, "xh", swap)
    served = exchange(picked, "y").reshape(NY * PIECE, LAT)
    keys = lax.all_gather(served, "zq", axis=0, tiled=True)
    own_latents, own_stats = own_attention(query, new_latents.reshape(ROWS, LAT))
    picks, all_gates = slots(routes.T, gates.T)
    slot_gates = lax.dynamic_slice_in_dim(all_gates, dev * OWN_SLOTS, OWN_SLOTS, 0)

    partial = exchange(prompt_attention(xh, all_queries, other_queries, keys), ("zl", "xh", "xl"))
    head_values = combine(partial, own_latents, own_stats, value_up)
    sums = exchange(add(exchange(project(head_values, out_weight), ("zl", "xh", "xl"))), "zq")
    rows = dispatch(zq, sums, picks).reshape(NEAR, OWN_SLOTS, SPAN)
    slot_rows = norm(exchange(rows, ("zl", "xh", "xl")), norm_gain.reshape(1, D))
    return (slot_rows[None], slot_gates.reshape(1, OWN_SLOTS // CAP, CAP))


def solution(mesh):
    axes = ("y", "core", "zq", "zl", "xh", "xl")
    fine = Mesh(mesh.devices.reshape(NY, 2, NQ, NL, 2, NX // 2), axes)
    group, dev = axes[:2], axes[2:]
    return jax.shard_map(
        local,
        mesh=fine,
        in_specs=(
            P(group, dev, None),
            P(),
            P(group, None, None, dev, None),
            P(group, None, None, None),
            P(dev, None, None),
            P(dev, None),
            P(),
            P(group, None),
            P(group, None),
        ),
        out_specs=(P(group, dev, None, None), P(group, dev, None)),
        check_vma=False,
    )
```

```python
import jax
import jax.numpy as jnp
from jax import lax
from jax.experimental import pallas as pl
from jax.experimental.pallas import tpu as pltpu
from jax.sharding import Mesh
from jax.sharding import PartitionSpec as P

D = 7168
LAT = 576
LAT_KV = 512
HEAD_V = 128
QK_DIM = 192
EXPERTS = 384
CAP = 2
ROWS = 64
EPSILON = 1e-06
SCALE = QK_DIM ** (-0.5)

NY, NQ, NL, NX = 8, 4, 2, 4
NEAR = NL * NX
DEVS = NQ * NEAR
PIECE = 192 // NY
KEYS = 192 * NQ
MINE = 2 * ROWS
LANES = LAT_KV // 128
STATS = LANES * MINE
SENT = STATS + 16
SLOTS = EXPERTS * CAP
OWN_SLOTS = SLOTS // DEVS
NEAR_SLOTS = NEAR * OWN_SLOTS
SPAN = D // NEAR
FOUR = 4
PACKED = LAT_KV // 128 * MINE + ROWS

bf16 = jnp.bfloat16
f32 = jnp.float32
VMEM = pl.BlockSpec(memory_space=pltpu.VMEM)
SMEM = pl.BlockSpec(memory_space=pltpu.SMEM)


def params(mib=24):
    return pltpu.CompilerParams(vmem_limit_bytes=mib * 1024 * 1024)


def cost(micros):
    return pl.CostEstimate(flops=0, bytes_accessed=3_000_000 * micros, transcendentals=0)


def dot(a, b, dims=((1,), (0,))):
    return lax.dot_general(a, b, (dims, ((), ())), preferred_element_type=f32)


def columns_to_lanes(column):
    return jnp.transpose(jnp.broadcast_to(column, (MINE, 128)))[:1]


def pick_kernel(core, wanted, mine, other, out):
    for y in range(NY):
        prompt = wanted[y]
        row = lax.shift_right_logical(prompt, 1)

        @pl.when((prompt & 1) == core[0])
        def _():
            out[y] = mine[row]

        @pl.when((prompt & 1) != core[0])
        def _():
            out[y] = other[row]


def pick(core, wanted, mine, other):
    return pl.pallas_call(
        pick_kernel,
        out_shape=jax.ShapeDtypeStruct(mine.shape, mine.dtype),
        in_specs=[SMEM, SMEM, VMEM, VMEM],
        out_specs=VMEM,
        compiler_params=params(),
        name="pick",
    )(core, wanted, mine, other)


def spread_kernel(query, copies, single):
    heads = [query[:, head, :] for head in range(2)]
    rest = jnp.concatenate([head[:, LAT_KV:] for head in heads], axis=1)
    for head in range(2):
        single[head * ROWS : (head + 1) * ROWS, :] = heads[head]
    for i in range(FOUR):
        for tile in range(LAT_KV // 128):
            for head in range(2):
                first = tile * MINE + head * ROWS
                copies[i, first : first + ROWS, :] = heads[head][:, tile * 128 : (tile + 1) * 128]
        copies[i, PACKED - ROWS :, :] = rest


def spread(query):
    return pl.pallas_call(
        spread_kernel,
        out_shape=(
            jax.ShapeDtypeStruct((FOUR, PACKED, 128), bf16),
            jax.ShapeDtypeStruct((MINE, LAT), bf16),
        ),
        in_specs=[VMEM],
        out_specs=(VMEM, VMEM),
        compiler_params=params(),
        cost_estimate=cost(2),
        name="spread",
    )(query)


def unpacked(packed, i):
    tiles = [packed[i, tile * MINE : (tile + 1) * MINE, :] for tile in range(LAT_KV // 128)]
    rest = packed[i, PACKED - ROWS :, :]
    width = LAT - LAT_KV
    tiles.append(jnp.concatenate([rest[:, :width], rest[:, width:]], axis=0))
    return jnp.concatenate(tiles, axis=1)


def attend(query, keys, visible=None):
    scores = dot(query, keys, ((1,), (1,))) * SCALE
    if visible is not None:
        scores = jnp.where(visible, scores, -1e30)
    best = jnp.max(scores, axis=1, keepdims=True)
    weights = jnp.exp(scores - best)
    total = jnp.sum(weights, axis=1, keepdims=True)
    latent = dot(weights.astype(bf16), keys[:, :LAT_KV]) * (1.0 / total)
    return best, total, latent.astype(bf16)


def three(value):
    high = value.astype(bf16).astype(f32)
    rest = value - high
    mid = rest.astype(bf16).astype(f32)
    return high, mid, rest - mid


def attention_kernel(xh, mine, other, keys, out):
    index = lax.broadcasted_iota(jnp.int32, (16, 128), 0)
    for step in range(1):
        query = jnp.concatenate(
            [unpacked(queries, i) for queries in (mine, other) for i in range(FOUR)], axis=0
        )
        best, total, latent = attend(query, keys[...])
        for i in range(2 * FOUR):
            part = slice(i * MINE, (i + 1) * MINE)
            owner = (xh[0] ^ (i // FOUR)) * 2 + (i % FOUR // 2) * NX + i % 2
            for tile in range(LANES):
                lanes = slice(tile * 128, (tile + 1) * 128)
                out[owner, tile * MINE : (tile + 1) * MINE, :] = latent[part, lanes]
            rows = three(columns_to_lanes(best[part])) + three(columns_to_lanes(total[part]))
            table = jnp.zeros((16, 128), f32)
            for j, row in enumerate(rows):
                table = jnp.where(index == j, jnp.broadcast_to(row, (16, 128)), table)
            out[owner, STATS:, :] = table.astype(bf16)


def prompt_attention(xh, mine, other, keys):
    return pl.pallas_call(
        attention_kernel,
        out_shape=jax.ShapeDtypeStruct((NEAR, SENT, 128), bf16),
        in_specs=[SMEM] + [VMEM] * 3,
        out_specs=VMEM,
        compiler_params=params(),
        name="prompt_attention",
    )(xh, mine, other, keys)


def own_kernel(query, keys, latents, stats):
    row = lax.broadcasted_iota(jnp.int32, (MINE, ROWS), 0) & (ROWS - 1)
    key = lax.broadcasted_iota(jnp.int32, (MINE, ROWS), 1)
    same = lax.shift_right_logical(row, 2) == lax.shift_right_logical(key, 2)
    best, total, latent = attend(query[...], keys[...], same & (key <= row))
    latents[...] = latent
    index = lax.broadcasted_iota(jnp.int32, (8, 128), 0)
    stats[...] = jnp.where(
        index == 0,
        jnp.broadcast_to(columns_to_lanes(best), (8, 128)),
        jnp.broadcast_to(columns_to_lanes(total), (8, 128)),
    )


def own_attention(query, keys):
    return pl.pallas_call(
        own_kernel,
        out_shape=(
            jax.ShapeDtypeStruct((MINE, LAT_KV), bf16),
            jax.ShapeDtypeStruct((8, 128), f32),
        ),
        in_specs=[VMEM] * 2,
        out_specs=(VMEM, VMEM),
        compiler_params=params(),
        name="own_attention",
    )(query, keys)


def combine_kernel(arrived, own_latents, own_stats, value_up, out):
    bests, totals = [own_stats[0:1, :]], [own_stats[1:2, :]]
    for z in range(NEAR):
        stats = arrived[z, STATS:, :].astype(f32)
        bests.append(stats[0:1] + stats[1:2] + stats[2:3])
        totals.append(stats[3:4] + stats[4:5] + stats[5:6])
    top = bests[0]
    for best in bests[1:]:
        top = jnp.maximum(top, best)
    shares = [total * jnp.exp(best - top) for best, total in zip(bests, totals)]
    whole = shares[0]
    for share in shares[1:]:
        whole = whole + share
    index = lax.broadcasted_iota(jnp.int32, (128, 128), 0)
    table = jnp.zeros((128, 128), f32)
    for i, share in enumerate(shares):
        table = jnp.where(index == i, jnp.broadcast_to(share / whole, (128, 128)), table)
    table = jnp.transpose(table)
    tiles = []
    for tile in range(LANES):
        lanes = slice(tile * 128, (tile + 1) * 128)
        latent = table[:, 0:1] * own_latents[:, lanes].astype(f32)
        for z in range(NEAR):
            part = arrived[z, tile * MINE : (tile + 1) * MINE, :].astype(f32)
            latent = latent + table[:, z + 1 : z + 2] * part
        tiles.append(latent.astype(bf16))
    latent = jnp.concatenate(tiles, axis=1)
    for head in range(2):
        values = dot(latent[head * ROWS : (head + 1) * ROWS], value_up[head])
        out[:, head * HEAD_V : (head + 1) * HEAD_V] = values.astype(bf16)


def combine(arrived, own_latents, own_stats, value_up):
    return pl.pallas_call(
        combine_kernel,
        out_shape=jax.ShapeDtypeStruct((ROWS, 2 * HEAD_V), bf16),
        in_specs=[VMEM] * 4,
        out_specs=VMEM,
        compiler_params=params(),
        name="combine",
    )(arrived, own_latents, own_stats, value_up)


def project_kernel(head_values, weight, out):
    for i in range(NEAR):
        out[i] = dot(head_values[...], weight[:, i * SPAN : (i + 1) * SPAN]).astype(bf16)


def project(head_values, weight):
    return pl.pallas_call(
        project_kernel,
        out_shape=jax.ShapeDtypeStruct((NEAR, ROWS, SPAN), bf16),
        in_specs=[VMEM] * 2,
        out_specs=VMEM,
        compiler_params=params(),
        name="project",
    )(head_values, weight)


def add_kernel(arrived, out):
    total = arrived[0].astype(f32)
    for i in range(1, NEAR):
        total = total + arrived[i].astype(f32)
    total = total.astype(bf16)
    for q in range(NQ):
        out[q] = total


def add(arrived):
    return pl.pallas_call(
        add_kernel,
        out_shape=jax.ShapeDtypeStruct((NQ, ROWS, SPAN), bf16),
        in_specs=[VMEM],
        out_specs=VMEM,
        compiler_params=params(),
        name="add",
    )(arrived)


def slots_kernel(routes, gates, picks, slot_gates):
    slot = lax.broadcasted_iota(jnp.int32, (SLOTS, ROWS), 0)
    expert = lax.shift_right_logical(slot, 1)
    chosen = jnp.zeros((SLOTS, ROWS), f32)
    gating = jnp.zeros((SLOTS, ROWS), f32)
    for k in range(8):
        match = expert == routes[k : k + 1, :]
        chosen = jnp.where(match, 1.0, chosen)
        gating = jnp.where(match, gates[k : k + 1, :], gating)
    earlier = lax.broadcasted_iota(jnp.int32, (ROWS, ROWS), 0) < lax.broadcasted_iota(
        jnp.int32, (ROWS, ROWS), 1
    )
    position = dot(chosen.astype(bf16), jnp.where(earlier, 1.0, 0.0).astype(bf16))
    place = (slot & 1).astype(f32)
    selected = jnp.where(position == place, chosen, 0.0)
    picks[...] = selected.astype(bf16)
    slot_gates[...] = jnp.sum(selected * gating, axis=1, keepdims=True)


def slots(routes, gates):
    return pl.pallas_call(
        slots_kernel,
        out_shape=(
            jax.ShapeDtypeStruct((SLOTS, ROWS), bf16),
            jax.ShapeDtypeStruct((SLOTS, 1), f32),
        ),
        in_specs=[VMEM] * 2,
        out_specs=(VMEM, VMEM),
        compiler_params=params(),
        name="slots",
    )(routes, gates)


def dispatch_kernel(zq, arrived, picks, out):
    total = arrived[0].astype(f32)
    for q in range(1, NQ):
        total = total + arrived[q].astype(f32)
    first = pl.multiple_of(zq[0] * NEAR_SLOTS, NEAR_SLOTS)
    out[...] = dot(picks[pl.ds(first, NEAR_SLOTS), :], total.astype(bf16)).astype(bf16)


def dispatch(zq, arrived, picks):
    return pl.pallas_call(
        dispatch_kernel,
        out_shape=jax.ShapeDtypeStruct((NEAR_SLOTS, SPAN), bf16),
        in_specs=[SMEM, VMEM, VMEM],
        out_specs=VMEM,
        compiler_params=params(),
        name="dispatch",
    )(zq, arrived, picks)


def norm_kernel(arrived, gain, out):
    square = jnp.zeros((OWN_SLOTS, 128), f32)
    for i in range(NEAR):
        block = arrived[i].astype(f32)
        for lane in range(0, SPAN, 128):
            part = block[:, lane : lane + 128]
            square = square + part * part
    scale = lax.rsqrt(jnp.sum(square, axis=1, keepdims=True) * (1.0 / D) + EPSILON)
    for i in range(NEAR):
        part = slice(i * SPAN, (i + 1) * SPAN)
        normed = arrived[i].astype(f32) * scale * gain[:, part].astype(f32)
        for expert in range(OWN_SLOTS // CAP):
            out[expert, :, part] = normed[expert * CAP : (expert + 1) * CAP]


def norm(arrived, gain):
    return pl.pallas_call(
        norm_kernel,
        out_shape=jax.ShapeDtypeStruct((OWN_SLOTS // CAP, CAP, D), f32),
        in_specs=[VMEM] * 2,
        out_specs=VMEM,
        compiler_params=params(),
        name="norm",
    )(arrived, gain)


def exchange(value, axes):
    return lax.all_to_all(value, axes, split_axis=0, concat_axis=0, tiled=True)


def local(
    prompt_cache,
    prompt_of_group,
    queries,
    new_latents,
    value_up,
    out_weight,
    norm_gain,
    routes,
    gates,
):
    core = lax.axis_index("core")[None].astype(jnp.int32)
    zq = lax.axis_index("zq")[None].astype(jnp.int32)
    xh = lax.axis_index("xh")[None].astype(jnp.int32)
    dev = (lax.axis_index("zq") * NL + lax.axis_index("zl")) * NX + (lax.axis_index("xh") * 2 + lax.axis_index("xl"))
    swap = [(0, 1), (1, 0)]

    copies, query = spread(queries.reshape(ROWS, 2, LAT))
    pieces = exchange(prompt_cache.reshape(NY, PIECE, LAT), "y")
    pieces, copies = lax.optimization_barrier((pieces, copies))
    all_queries = exchange(copies, ("zl", "xl"))
    other = lax.ppermute(pieces, "core", swap)
    wanted = jnp.where(core[0] == 0, prompt_of_group[0::2], prompt_of_group[1::2])
    picked = pick(core, wanted, pieces, other)
    picked, all_queries = lax.optimization_barrier((picked, all_queries))
    other_queries = lax.ppermute(all_queries, "xh", swap)
    served = exchange(picked, "y").reshape(NY * PIECE, LAT)
    keys = lax.all_gather(served, "zq", axis=0, tiled=True)
    own_latents, own_stats = own_attention(query, new_latents.reshape(ROWS, LAT))
    picks, all_gates = slots(routes.T, gates.T)
    slot_gates = lax.dynamic_slice_in_dim(all_gates, dev * OWN_SLOTS, OWN_SLOTS, 0)

    partial = exchange(prompt_attention(xh, all_queries, other_queries, keys), ("zl", "xh", "xl"))
    head_values = combine(partial, own_latents, own_stats, value_up)
    sums = exchange(add(exchange(project(head_values, out_weight), ("zl", "xh", "xl"))), "zq")
    rows = dispatch(zq, sums, picks).reshape(NEAR, OWN_SLOTS, SPAN)
    slot_rows = norm(exchange(rows, ("zl", "xh", "xl")), norm_gain.reshape(1, D))
    return (slot_rows[None], slot_gates.reshape(1, OWN_SLOTS // CAP, CAP))


def solution(mesh):
    axes = ("y", "core", "zq", "zl", "xh", "xl")
    fine = Mesh(mesh.devices.reshape(NY, 2, NQ, NL, 2, NX // 2), axes)
    group, dev = axes[:2], axes[2:]
    return jax.shard_map(
        local,
        mesh=fine,
        in_specs=(
            P(group, dev, None),
            P(),
            P(group, None, None, dev, None),
            P(group, None, None, None),
            P(dev, None, None),
            P(dev, None),
            P(),
            P(group, None),
            P(group, None),
        ),
        out_specs=(P(group, dev, None, None), P(group, dev, None)),
        check_vma=False,
    )
```

```python
import jax
import jax.numpy as jnp
from jax import lax
from jax.experimental import pallas as pl
from jax.experimental.pallas import tpu as pltpu
from jax.sharding import Mesh
from jax.sharding import PartitionSpec as P

D = 7168
LAT = 576
LAT_KV = 512
HEAD_V = 128
QK_DIM = 192
EXPERTS = 384
CAP = 2
ROWS = 64
EPSILON = 1e-06
SCALE = QK_DIM ** (-0.5)

NY, NQ, NL, NX = 8, 4, 2, 4
NEAR = NL * NX
DEVS = NQ * NEAR
PIECE = 192 // NY
KEYS = 192 * NQ
MINE = 2 * ROWS
LANES = LAT_KV // 128
STATS = LANES * MINE
SENT = STATS + 16
SLOTS = EXPERTS * CAP
OWN_SLOTS = SLOTS // DEVS
NEAR_SLOTS = NEAR * OWN_SLOTS
SPAN = D // NEAR
FOUR = 4
PACKED = LAT_KV // 128 * MINE + ROWS

bf16 = jnp.bfloat16
f32 = jnp.float32
VMEM = pl.BlockSpec(memory_space=pltpu.VMEM)
SMEM = pl.BlockSpec(memory_space=pltpu.SMEM)


def params(mib=24):
    return pltpu.CompilerParams(vmem_limit_bytes=mib * 1024 * 1024)


def cost(micros):
    return pl.CostEstimate(flops=0, bytes_accessed=3_000_000 * micros, transcendentals=0)


def dot(a, b, dims=((1,), (0,))):
    return lax.dot_general(a, b, (dims, ((), ())), preferred_element_type=f32)


def columns_to_lanes(column):
    return jnp.transpose(jnp.broadcast_to(column, (MINE, 128)))[:1]


def pick_kernel(core, wanted, mine, other, out, sems):
    for y in range(NY):
        prompt = wanted[y]
        row = lax.shift_right_logical(prompt, 1)

        @pl.when((prompt & 1) == core[0])
        def _():
            pltpu.make_async_copy(mine.at[row], out.at[y], sems.at[y]).start()

        @pl.when((prompt & 1) != core[0])
        def _():
            pltpu.make_async_copy(other.at[row], out.at[y], sems.at[y]).start()

    for y in range(NY):
        pltpu.make_async_copy(mine.at[0], out.at[y], sems.at[y]).wait()


def pick(core, wanted, mine, other):
    return pl.pallas_call(
        pick_kernel,
        out_shape=jax.ShapeDtypeStruct(mine.shape, mine.dtype),
        in_specs=[SMEM, SMEM] + [pl.BlockSpec(memory_space=pl.ANY)] * 2,
        out_specs=pl.BlockSpec(memory_space=pl.ANY),
        scratch_shapes=[pltpu.SemaphoreType.DMA((NY,))],
        compiler_params=params(),
        name="pick",
    )(core, wanted, mine, other)


def spread_kernel(query, copies, single):
    heads = [query[:, head, :] for head in range(2)]
    rest = jnp.concatenate([head[:, LAT_KV:] for head in heads], axis=1)
    for head in range(2):
        single[head * ROWS : (head + 1) * ROWS, :] = heads[head]
    for i in range(FOUR):
        for tile in range(LAT_KV // 128):
            for head in range(2):
                first = tile * MINE + head * ROWS
                copies[i, first : first + ROWS, :] = heads[head][:, tile * 128 : (tile + 1) * 128]
        copies[i, PACKED - ROWS :, :] = rest


def spread(query):
    return pl.pallas_call(
        spread_kernel,
        out_shape=(
            jax.ShapeDtypeStruct((FOUR, PACKED, 128), bf16),
            jax.ShapeDtypeStruct((MINE, LAT), bf16),
        ),
        in_specs=[VMEM],
        out_specs=(VMEM, VMEM),
        compiler_params=params(),
        cost_estimate=cost(2),
        name="spread",
    )(query)


def unpacked(packed, i):
    tiles = [packed[i, tile * MINE : (tile + 1) * MINE, :] for tile in range(LAT_KV // 128)]
    rest = packed[i, PACKED - ROWS :, :]
    width = LAT - LAT_KV
    tiles.append(jnp.concatenate([rest[:, :width], rest[:, width:]], axis=0))
    return jnp.concatenate(tiles, axis=1)


def attend(query, keys, visible=None):
    scores = dot(query, keys, ((1,), (1,))) * SCALE
    if visible is not None:
        scores = jnp.where(visible, scores, -1e30)
    best = jnp.max(scores, axis=1, keepdims=True)
    weights = jnp.exp(scores - best)
    total = jnp.sum(weights, axis=1, keepdims=True)
    latent = dot(weights.astype(bf16), keys[:, :LAT_KV]) * (1.0 / total)
    return best, total, latent.astype(bf16)


def three(value):
    high = value.astype(bf16).astype(f32)
    rest = value - high
    mid = rest.astype(bf16).astype(f32)
    return high, mid, rest - mid


def attention_kernel(xh, mine, other, keys, out):
    index = lax.broadcasted_iota(jnp.int32, (16, 128), 0)
    for step in range(1):
        query = jnp.concatenate(
            [unpacked(queries, i) for queries in (mine, other) for i in range(FOUR)], axis=0
        )
        best, total, latent = attend(query, keys[...])
        for i in range(2 * FOUR):
            part = slice(i * MINE, (i + 1) * MINE)
            owner = (xh[0] ^ (i // FOUR)) * 2 + (i % FOUR // 2) * NX + i % 2
            for tile in range(LANES):
                lanes = slice(tile * 128, (tile + 1) * 128)
                out[owner, tile * MINE : (tile + 1) * MINE, :] = latent[part, lanes]
            rows = three(columns_to_lanes(best[part])) + three(columns_to_lanes(total[part]))
            table = jnp.zeros((16, 128), f32)
            for j, row in enumerate(rows):
                table = jnp.where(index == j, jnp.broadcast_to(row, (16, 128)), table)
            out[owner, STATS:, :] = table.astype(bf16)


def prompt_attention(xh, mine, other, keys):
    return pl.pallas_call(
        attention_kernel,
        out_shape=jax.ShapeDtypeStruct((NEAR, SENT, 128), bf16),
        in_specs=[SMEM] + [VMEM] * 3,
        out_specs=VMEM,
        compiler_params=params(),
        name="prompt_attention",
    )(xh, mine, other, keys)


def own_kernel(query, keys, latents, stats):
    row = lax.broadcasted_iota(jnp.int32, (MINE, ROWS), 0) & (ROWS - 1)
    key = lax.broadcasted_iota(jnp.int32, (MINE, ROWS), 1)
    same = lax.shift_right_logical(row, 2) == lax.shift_right_logical(key, 2)
    best, total, latent = attend(query[...], keys[...], same & (key <= row))
    latents[...] = latent
    index = lax.broadcasted_iota(jnp.int32, (8, 128), 0)
    stats[...] = jnp.where(
        index == 0,
        jnp.broadcast_to(columns_to_lanes(best), (8, 128)),
        jnp.broadcast_to(columns_to_lanes(total), (8, 128)),
    )


def own_attention(query, keys):
    return pl.pallas_call(
        own_kernel,
        out_shape=(
            jax.ShapeDtypeStruct((MINE, LAT_KV), bf16),
            jax.ShapeDtypeStruct((8, 128), f32),
        ),
        in_specs=[VMEM] * 2,
        out_specs=(VMEM, VMEM),
        compiler_params=params(),
        name="own_attention",
    )(query, keys)


def combine_kernel(arrived, own_latents, own_stats, value_up, out):
    bests, totals = [own_stats[0:1, :]], [own_stats[1:2, :]]
    for z in range(NEAR):
        stats = arrived[z, STATS:, :].astype(f32)
        bests.append(stats[0:1] + stats[1:2] + stats[2:3])
        totals.append(stats[3:4] + stats[4:5] + stats[5:6])
    top = bests[0]
    for best in bests[1:]:
        top = jnp.maximum(top, best)
    shares = [total * jnp.exp(best - top) for best, total in zip(bests, totals)]
    whole = shares[0]
    for share in shares[1:]:
        whole = whole + share
    index = lax.broadcasted_iota(jnp.int32, (128, 128), 0)
    table = jnp.zeros((128, 128), f32)
    for i, share in enumerate(shares):
        table = jnp.where(index == i, jnp.broadcast_to(share / whole, (128, 128)), table)
    table = jnp.transpose(table)
    tiles = []
    for tile in range(LANES):
        lanes = slice(tile * 128, (tile + 1) * 128)
        latent = table[:, 0:1] * own_latents[:, lanes].astype(f32)
        for z in range(NEAR):
            part = arrived[z, tile * MINE : (tile + 1) * MINE, :].astype(f32)
            latent = latent + table[:, z + 1 : z + 2] * part
        tiles.append(latent.astype(bf16))
    latent = jnp.concatenate(tiles, axis=1)
    for head in range(2):
        values = dot(latent[head * ROWS : (head + 1) * ROWS], value_up[head])
        out[:, head * HEAD_V : (head + 1) * HEAD_V] = values.astype(bf16)


def combine(arrived, own_latents, own_stats, value_up):
    return pl.pallas_call(
        combine_kernel,
        out_shape=jax.ShapeDtypeStruct((ROWS, 2 * HEAD_V), bf16),
        in_specs=[VMEM] * 4,
        out_specs=VMEM,
        compiler_params=params(),
        name="combine",
    )(arrived, own_latents, own_stats, value_up)


def project_kernel(head_values, weight, out):
    for i in range(NEAR):
        out[i] = dot(head_values[...], weight[:, i * SPAN : (i + 1) * SPAN]).astype(bf16)


def project(head_values, weight):
    return pl.pallas_call(
        project_kernel,
        out_shape=jax.ShapeDtypeStruct((NEAR, ROWS, SPAN), bf16),
        in_specs=[VMEM] * 2,
        out_specs=VMEM,
        compiler_params=params(),
        name="project",
    )(head_values, weight)


def add_kernel(arrived, out):
    total = arrived[0].astype(f32)
    for i in range(1, NEAR):
        total = total + arrived[i].astype(f32)
    total = total.astype(bf16)
    for q in range(NQ):
        out[q] = total


def add(arrived):
    return pl.pallas_call(
        add_kernel,
        out_shape=jax.ShapeDtypeStruct((NQ, ROWS, SPAN), bf16),
        in_specs=[VMEM],
        out_specs=VMEM,
        compiler_params=params(),
        name="add",
    )(arrived)


def slots_kernel(routes, gates, picks, slot_gates):
    slot = lax.broadcasted_iota(jnp.int32, (SLOTS, ROWS), 0)
    expert = lax.shift_right_logical(slot, 1)
    chosen = jnp.zeros((SLOTS, ROWS), f32)
    gating = jnp.zeros((SLOTS, ROWS), f32)
    for k in range(8):
        match = expert == routes[k : k + 1, :]
        chosen = jnp.where(match, 1.0, chosen)
        gating = jnp.where(match, gates[k : k + 1, :], gating)
    earlier = lax.broadcasted_iota(jnp.int32, (ROWS, ROWS), 0) < lax.broadcasted_iota(
        jnp.int32, (ROWS, ROWS), 1
    )
    position = dot(chosen.astype(bf16), jnp.where(earlier, 1.0, 0.0).astype(bf16))
    place = (slot & 1).astype(f32)
    selected = jnp.where(position == place, chosen, 0.0)
    picks[...] = selected.astype(bf16)
    slot_gates[...] = jnp.sum(selected * gating, axis=1, keepdims=True)


def slots(routes, gates):
    return pl.pallas_call(
        slots_kernel,
        out_shape=(
            jax.ShapeDtypeStruct((SLOTS, ROWS), bf16),
            jax.ShapeDtypeStruct((SLOTS, 1), f32),
        ),
        in_specs=[VMEM] * 2,
        out_specs=(VMEM, VMEM),
        compiler_params=params(),
        name="slots",
    )(routes, gates)


def dispatch_kernel(zq, arrived, picks, out):
    total = arrived[0].astype(f32)
    for q in range(1, NQ):
        total = total + arrived[q].astype(f32)
    first = pl.multiple_of(zq[0] * NEAR_SLOTS, NEAR_SLOTS)
    out[...] = dot(picks[pl.ds(first, NEAR_SLOTS), :], total.astype(bf16)).astype(bf16)


def dispatch(zq, arrived, picks):
    return pl.pallas_call(
        dispatch_kernel,
        out_shape=jax.ShapeDtypeStruct((NEAR_SLOTS, SPAN), bf16),
        in_specs=[SMEM, VMEM, VMEM],
        out_specs=VMEM,
        compiler_params=params(),
        name="dispatch",
    )(zq, arrived, picks)


def norm_kernel(arrived, gain, out):
    square = jnp.zeros((OWN_SLOTS, 128), f32)
    for i in range(NEAR):
        block = arrived[i].astype(f32)
        for lane in range(0, SPAN, 128):
            part = block[:, lane : lane + 128]
            square = square + part * part
    scale = lax.rsqrt(jnp.sum(square, axis=1, keepdims=True) * (1.0 / D) + EPSILON)
    for i in range(NEAR):
        part = slice(i * SPAN, (i + 1) * SPAN)
        normed = arrived[i].astype(f32) * scale * gain[:, part].astype(f32)
        for expert in range(OWN_SLOTS // CAP):
            out[expert, :, part] = normed[expert * CAP : (expert + 1) * CAP]


def norm(arrived, gain):
    return pl.pallas_call(
        norm_kernel,
        out_shape=jax.ShapeDtypeStruct((OWN_SLOTS // CAP, CAP, D), f32),
        in_specs=[VMEM] * 2,
        out_specs=VMEM,
        compiler_params=params(),
        name="norm",
    )(arrived, gain)


def exchange(value, axes):
    return lax.all_to_all(value, axes, split_axis=0, concat_axis=0, tiled=True)


def local(
    prompt_cache,
    prompt_of_group,
    queries,
    new_latents,
    value_up,
    out_weight,
    norm_gain,
    routes,
    gates,
):
    core = lax.axis_index("core")[None].astype(jnp.int32)
    zq = lax.axis_index("zq")[None].astype(jnp.int32)
    xh = lax.axis_index("xh")[None].astype(jnp.int32)
    dev = (lax.axis_index("zq") * NL + lax.axis_index("zl")) * NX + (lax.axis_index("xh") * 2 + lax.axis_index("xl"))
    swap = [(0, 1), (1, 0)]

    copies, query = spread(queries.reshape(ROWS, 2, LAT))
    pieces = exchange(prompt_cache.reshape(NY, PIECE, LAT), "y")
    pieces, copies = lax.optimization_barrier((pieces, copies))
    all_queries = exchange(copies, ("zl", "xl"))
    other = lax.ppermute(pieces, "core", swap)
    wanted = jnp.where(core[0] == 0, prompt_of_group[0::2], prompt_of_group[1::2])
    picked = pick(core, wanted, pieces, other)
    picked, all_queries = lax.optimization_barrier((picked, all_queries))
    other_queries = lax.ppermute(all_queries, "xh", swap)
    served = exchange(picked, "y").reshape(NY * PIECE, LAT)
    keys = lax.all_gather(served, "zq", axis=0, tiled=True)
    own_latents, own_stats = own_attention(query, new_latents.reshape(ROWS, LAT))
    picks, all_gates = slots(routes.T, gates.T)
    slot_gates = lax.dynamic_slice_in_dim(all_gates, dev * OWN_SLOTS, OWN_SLOTS, 0)

    partial = exchange(prompt_attention(xh, all_queries, other_queries, keys), ("zl", "xh", "xl"))
    head_values = combine(partial, own_latents, own_stats, value_up)
    sums = exchange(add(exchange(project(head_values, out_weight), ("zl", "xh", "xl"))), "zq")
    rows = dispatch(zq, sums, picks).reshape(NEAR, OWN_SLOTS, SPAN)
    slot_rows = norm(exchange(rows, ("zl", "xh", "xl")), norm_gain.reshape(1, D))
    return (slot_rows[None], slot_gates.reshape(1, OWN_SLOTS // CAP, CAP))


def solution(mesh):
    axes = ("y", "core", "zq", "zl", "xh", "xl")
    fine = Mesh(mesh.devices.reshape(NY, 2, NQ, NL, 2, NX // 2), axes)
    group, dev = axes[:2], axes[2:]
    return jax.shard_map(
        local,
        mesh=fine,
        in_specs=(
            P(group, dev, None),
            P(),
            P(group, None, None, dev, None),
            P(group, None, None, None),
            P(dev, None, None),
            P(dev, None),
            P(),
            P(group, None),
            P(group, None),
        ),
        out_specs=(P(group, dev, None, None), P(group, dev, None)),
        check_vma=False,
    )
```
